32 devices in a mesh: fsdp: 8 (over z, y), ctx: 4 (over x, core).
Axes of the slice: x: 2, y: 2, z: 4, core: 2. Of those that a mesh axis runs over, the one named last changes fastest.
Arguments:
- inputs: bfloat16 [8, 1024, 768], P('fsdp', 'ctx'), may hold values from -8 to 8
- cotangent: bfloat16 [8, 1024, 768], P('fsdp', 'ctx'), may hold values from -8 to 8
- block_order: int32 [8], replicated, may hold values from 0 to 7, each once
- norm1_gain: bfloat16 [768], P('fsdp'), may hold values from 0.5 to 1.5
- norm1_shift: bfloat16 [768], P('fsdp'), may hold values from -1.25 to 1.25
- w_qkv: bfloat16 [768, 2304], P('fsdp'), may hold values from -0.21875 to 0.21875
- qv_bias: bfloat16 [2, 768], P(None, 'fsdp'), may hold values from -1.75 to 1.75
- w_out: bfloat16 [768, 768], P('fsdp'), may hold values from -1.75 to 1.75
- out_bias: bfloat16 [768], P('fsdp'), may hold values from -1.25 to 1.25
- norm2_gain: bfloat16 [768], P('fsdp'), may hold values from 0.5 to 1.5
- norm2_shift: bfloat16 [768], P('fsdp'), may hold values from -1.25 to 1.25
- w_fc: bfloat16 [768, 3072], P('fsdp'), may hold values from -0.21875 to 0.21875
- fc_bias: bfloat16 [3072], P('fsdp'), may hold values from -3 to 3
- w_proj: bfloat16 [3072, 768], P('fsdp'), may hold values from -0.109375 to 0.109375
- proj_bias: bfloat16 [768], P('fsdp'), may hold values from -1.25 to 1.25
Outputs:
- output: bfloat16 [8, 1024, 768], P('fsdp', 'ctx')
- input_grad: bfloat16 [8, 1024, 768], P('fsdp', 'ctx')
- norm1_gain_grad: float32 [768], P('fsdp')
- norm1_shift_grad: float32 [768], P('fsdp')
- w_qkv_grad: float32 [768, 2304], P('fsdp')
- qv_bias_grad: float32 [2, 768], P(None, 'fsdp')
- w_out_grad: float32 [768, 768], P('fsdp')
- out_bias_grad: float32 [768], P('fsdp')
- norm2_gain_grad: float32 [768], P('fsdp')
- norm2_shift_grad: float32 [768], P('fsdp')
- w_fc_grad: float32 [768, 3072], P('fsdp')
- fc_bias_grad: float32 [3072], P('fsdp')
- w_proj_grad: float32 [3072, 768], P('fsdp')
- proj_bias_grad: float32 [768], P('fsdp')
The draws below stay inside these ranges and needn't reach their ends.
Inputs may be any that keep to these rules, and one draw needn't show every extreme that they name: block_order names each of the 128-token position blocks of a sequence once.
All inputs are finite; a program needn't handle non-finite values.
Results may differ from the reference program's by a relative error of at most 0.02.
Values may be sent and summed in bfloat16 or wider, within the bound.
A program may use at most 128 MiB of HBM per device.

```python
import jax
import jax.numpy as jnp
from jax import lax

D = 768
HEADS = 12
HEAD_DIM = 64
FF = 3072
LEN = 1024
SEQS = 8
N_CTX = 4


def spiked(array, rng, source, target, blocks, factor):
    def block_of(axis_at):
        return (jnp.arange(array.shape[axis_at]) // (array.shape[axis_at] // blocks)).reshape((-1,) + (1,) * (array.ndim - 1 - axis_at))

    near = jax.random.permutation(rng, blocks)[block_of(target)]
    second = (block_of(target) + blocks // 2) % blocks
    return jnp.where((block_of(source) == near) | (block_of(source) == second), factor * array, array)


def block_scale(rng, extent, split, smallest, high):
    level = 1.0
    for dim, blocks in split:
        draws = jax.random.uniform(jax.random.fold_in(jax.random.fold_in(rng, 6), dim), (blocks,), jnp.float32, smallest / len(split), high / len(split))
        level = level * jnp.repeat(jnp.exp(draws), extent[dim] // blocks).reshape((-1,) + (1,) * (len(extent) - 1 - dim))
    return level


def scatter_about(key, shape, width, reach, split=(), kind=jnp.bfloat16):
    array = jax.random.normal(key, shape, jnp.float32) * width
    if len(split) > 0:
        array = block_scale(key, shape, split, -0.22, 0.18) * array
    return jnp.clip(array, min=-reach, max=reach).astype(kind)


def heavy_noise(key, dims, scale, reach, pieces, heavy, kind=jnp.bfloat16):
    entries = scale * jax.random.normal(key, dims, jnp.float32)
    if pieces:
        entries = entries * block_scale(key, dims, pieces, -0.22, 0.18)
    return jnp.clip(spiked(entries, jax.random.fold_in(key, 3), *heavy), -reach, reach).astype(kind)


def setup_inputs(seed: int = 0) -> dict:
    key_list = jax.random.split(jax.random.key(seed), 16)
    inputs = heavy_noise(key_list[0], (SEQS, LEN, D), 1.0, 8.0, ((0, 8), (1, 4)), (0, 2, 8, 2.0))
    cotangent = heavy_noise(key_list[1], (SEQS, LEN, D), 1.0, 8.0, ((0, 8), (1, 4)), (0, 2, 8, 2.0))
    block_order = jax.random.permutation(key_list[2], 2 * N_CTX).astype(jnp.int32)
    norm1_gain = jnp.clip(1.0 + 0.1 * jax.random.normal(key_list[3], (D,), jnp.float32), 0.5, 1.5).astype(jnp.bfloat16)
    norm1_shift = scatter_about(key_list[4], (D,), 0.2, 1.25, ((0, 8),))
    w_qkv = scatter_about(key_list[5], (D, 3 * D), D ** -0.5, 0.21875, ((0, 8),))
    qv_bias = scatter_about(key_list[6], (2, D), 0.3, 1.75, ((1, 8),))
    w_out = scatter_about(key_list[7], (D, D), (max(D // 64, 1)) ** -0.5, 1.75, ((0, 8),))
    out_bias = scatter_about(key_list[8], (D,), 0.2, 1.25, ((0, 8),))
    norm2_gain = jnp.clip(1.0 + 0.1 * jax.random.normal(key_list[9], (D,), jnp.float32), 0.5, 1.5).astype(jnp.bfloat16)
    norm2_shift = scatter_about(key_list[10], (D,), 0.2, 1.25, ((0, 8),))
    w_fc = scatter_about(key_list[11], (D, FF), D ** -0.5, 0.21875, ((0, 8),))
    fc_bias = scatter_about(key_list[12], (FF,), 0.5, 3.0, ((0, 8),))
    w_proj = scatter_about(key_list[13], (FF, D), FF ** -0.5, 0.109375, ((0, 8),))
    proj_bias = scatter_about(key_list[14], (D,), 0.2, 1.25, ((0, 8),))
    return dict(inputs=inputs, cotangent=cotangent, block_order=block_order, norm1_gain=norm1_gain, norm1_shift=norm1_shift, w_qkv=w_qkv, qv_bias=qv_bias, w_out=w_out, out_bias=out_bias, norm2_gain=norm2_gain, norm2_shift=norm2_shift, w_fc=w_fc, fc_bias=fc_bias, w_proj=w_proj, proj_bias=proj_bias)


EPS = 1e-05
HIGH = lax.Precision.HIGHEST

@jax.custom_vjp
def low(v):
    return lax.optimization_barrier(v.astype(jnp.bfloat16)).astype(jnp.float32)

@jax.custom_vjp
def low_back(v):
    return v

def low_keep(v):
    return (low(v), None)

def low_pass(kept, grad):
    return (grad,)

def back_keep(v):
    return (v, None)

def back_low(kept, grad):
    return (low(grad),)
low.defvjp(low_keep, low_pass)
low_back.defvjp(back_keep, back_low)

def layer_norm(values, gain, shift):
    centre = lax.optimization_barrier(jnp.mean(values, axis=-1, keepdims=True))
    centred = values - centre
    spread = lax.optimization_barrier(jnp.mean(centred * centred, axis=-1, keepdims=True))
    return centred * lax.rsqrt(spread + EPS) * gain + shift

def storage_places(block_order, length):
    block_rows = length // block_order.shape[0]
    row_index = jnp.arange(length, dtype=jnp.int32)
    return block_order[row_index // block_rows] * block_rows + row_index % block_rows

def one_sequence(params, tokens, places):
    norm1_gain, norm1_shift, w_qkv, qv_bias, w_out, out_bias, norm2_gain, norm2_shift, w_fc, fc_bias, w_proj, proj_bias = params
    length = tokens.shape[0]
    score_scale = HEAD_DIM ** (-0.5)
    normed_one = low(layer_norm(tokens, norm1_gain, norm1_shift))
    qkv_shift = jnp.concatenate([qv_bias[0], jnp.zeros_like(qv_bias[0]), qv_bias[1]])
    qkv_all = low(low_back(jnp.dot(normed_one, w_qkv, precision=HIGH) + qkv_shift))
    queries = qkv_all[:, :D].reshape(length, HEADS, HEAD_DIM)
    key_rows = qkv_all[:, D:2 * D].reshape(length, HEADS, HEAD_DIM)
    value_rows = qkv_all[:, 2 * D:].reshape(length, HEADS, HEAD_DIM)
    block_span = min(512, length)

    def attend(block_index):
        first_row = block_index * block_span
        block_queries = lax.dynamic_slice_in_dim(queries, first_row, block_span, 0)
        query_places = lax.dynamic_slice_in_dim(places, first_row, block_span, 0)
        scores = low_back(jnp.einsum('thd,shd->hts', block_queries, key_rows, precision=HIGH) * score_scale)
        visible = places[None, None, :] <= query_places[None, :, None]
        scores = jnp.where(visible, scores, -jnp.inf)
        highest = lax.optimization_barrier(jnp.max(scores, axis=-1, keepdims=True))
        weights = jnp.exp(scores - highest)
        shares = low(weights / lax.optimization_barrier(jnp.sum(weights, axis=-1, keepdims=True)))
        return jnp.einsum('hts,shd->thd', shares, value_rows, precision=HIGH)
    attended = lax.map(jax.checkpoint(attend), jnp.arange(length // block_span))
    attended = low(low_back(attended.reshape(length, D)))
    branch = low_back(jnp.dot(attended, w_out, precision=HIGH) + out_bias)
    middle = tokens + branch
    normed_two = low(layer_norm(middle, norm2_gain, norm2_shift))
    hidden = low_back(jnp.dot(normed_two, w_fc, precision=HIGH) + fc_bias)
    activated = low(jax.nn.gelu(hidden, approximate=True))
    return middle + jnp.dot(activated, w_proj, precision=HIGH) + proj_bias

def reference(inputs, cotangent, block_order, norm1_gain, norm1_shift, w_qkv, qv_bias, w_out, out_bias, norm2_gain, norm2_shift, w_fc, fc_bias, w_proj, proj_bias):
    params = jax.tree.map(lambda element: element.astype(jnp.float32), (norm1_gain, norm1_shift, w_qkv, qv_bias, w_out, out_bias, norm2_gain, norm2_shift, w_fc, fc_bias, w_proj, proj_bias))
    places = storage_places(block_order, inputs.shape[1])

    def forward(tokens_all, weights_all):

        def per_sequence(tokens):
            return one_sequence(weights_all, tokens, places)
        return lax.map(jax.checkpoint(per_sequence), tokens_all)
    outputs, pullback = jax.vjp(forward, inputs.astype(jnp.float32), params)
    input_grad, grads = pullback(cotangent.astype(jnp.float32))
    return (outputs.astype(jnp.bfloat16), input_grad.astype(jnp.bfloat16), grads[0], grads[1], grads[2], grads[3], grads[4], grads[5], grads[6], grads[7], grads[8], grads[9], grads[10], grads[11])
```

```python
import jax
import jax.numpy as jnp
from jax import lax
from jax.experimental import pallas as pl
from jax.experimental.pallas import tpu as pltpu
from jax.sharding import PartitionSpec as P

HEADS = 12
EPS = 1e-05
LOWEST = -1e30
LANES = 128
F32 = jnp.float32
BF16 = jnp.bfloat16
ROW_DOT = (((0,), (0,)), ((), ()))
LANE_DOT = (((1,), (1,)), ((), ()))


def dot(left, right):
    return jnp.dot(left, right, preferred_element_type=F32)


def dot_rows(left, right):
    return lax.dot_general(left, right, ROW_DOT, preferred_element_type=F32)


def dot_lanes(left, right):
    return lax.dot_general(left, right, LANE_DOT, preferred_element_type=F32)


def normalise(values):
    centred = values - jnp.mean(values, axis=-1, keepdims=True)
    spread = jnp.mean(centred * centred, axis=-1, keepdims=True)
    inverse = lax.rsqrt(spread + EPS)
    return centred * inverse, inverse


def norm_backward(incoming, gain, unit, inverse):
    scaled = incoming * gain
    first = jnp.mean(scaled, axis=-1, keepdims=True)
    second = jnp.mean(scaled * unit, axis=-1, keepdims=True)
    return inverse * (scaled - first - unit * second)


def gelu_pair(values):
    inner = 0.7978845608028654 * (values + 0.044715 * values * values * values)
    bent = jnp.tanh(inner)
    slope = 0.7978845608028654 * (1.0 + 0.134145 * values * values)
    value = 0.5 * values * (1.0 + bent)
    derivative = 0.5 * (1.0 + bent) + 0.5 * values * (1.0 - bent * bent) * slope
    return value, derivative


def block_places(block_order, first_row, row_count, block_rows):
    row_index = first_row + jnp.arange(row_count, dtype=jnp.int32)
    which_block = row_index // block_rows
    table = jnp.arange(block_order.shape[0], dtype=jnp.int32)
    picked = jnp.sum(
        jnp.where(which_block[:, None] == table[None, :], block_order[None, :], 0), axis=1
    )
    return picked * block_rows + row_index % block_rows


def attend_kernel(query_place, key_place, q_ref, kv_ref, out_ref, log_ref):
    rows, width = q_ref.shape
    head_dim = width // HEADS
    per_group = LANES // head_dim
    visible = key_place[...] <= query_place[...]
    lane = lax.broadcasted_iota(jnp.int32, (rows, LANES), 1)
    logs = jnp.zeros((rows, LANES), F32)
    for group in range(width // LANES):
        span = pl.ds(group * LANES, LANES)
        q = q_ref[:, span] * (head_dim**-0.5)
        k = kv_ref[:, span]
        v = kv_ref[:, pl.ds(width + group * LANES, LANES)]
        out = jnp.zeros((rows, LANES), F32)
        for part in range(per_group):
            own = lane // head_dim == part
            scores = dot_lanes(jnp.where(own, q, jnp.zeros_like(q)), k)
            scores = jnp.where(visible, scores, LOWEST)
            high = jnp.max(scores, axis=1, keepdims=True)
            shares = jnp.exp(scores - high)
            total = jnp.sum(shares, axis=1, keepdims=True)
            out = jnp.where(own, dot(shares.astype(BF16), v) / total, out)
            logs = jnp.where(lane == group * per_group + part, high + jnp.log(total), logs)
        out_ref[:, span] = out
    log_ref[...] = logs


def attend_back_kernel(
    query_place, key_place, q_ref, kv_ref, att_ref, grad_ref, log_ref, dq_ref, dkv_ref
):
    rows, width = q_ref.shape
    head_dim = width // HEADS
    per_group = LANES // head_dim
    scale = head_dim**-0.5
    visible = key_place[...] <= query_place[...]
    lane = lax.broadcasted_iota(jnp.int32, (rows, LANES), 1)
    for group in range(width // LANES):
        span = pl.ds(group * LANES, LANES)
        far = pl.ds(width + group * LANES, LANES)
        q = q_ref[:, span] * scale
        k = kv_ref[:, span]
        v = kv_ref[:, far]
        grad = grad_ref[:, span]
        product = grad.astype(F32) * att_ref[:, span]
        dq = jnp.zeros((rows, LANES), F32)
        dk = jnp.zeros((k.shape[0], LANES), F32)
        dv = jnp.zeros((k.shape[0], LANES), F32)
        for part in range(per_group):
            own = lane // head_dim == part
            own_q = jnp.where(own, q, jnp.zeros_like(q))
            own_grad = jnp.where(own, grad, jnp.zeros_like(grad))
            delta = jnp.sum(jnp.where(own, product, 0.0), axis=1, keepdims=True)
            log = jnp.sum(
                jnp.where(lane == group * per_group + part, log_ref[...], 0.0),
                axis=1,
                keepdims=True,
            )
            scores = jnp.where(visible, dot_lanes(own_q, k), LOWEST)
            shares = jnp.exp(scores - log)
            dv = dv + dot_rows(shares.astype(BF16), own_grad)
            change = (shares * (dot_lanes(own_grad, v) - delta)).astype(BF16)
            dq = jnp.where(own, dot(change, k) * scale, dq)
            dk = dk + dot_rows(change, own_q)
        dq_ref[:, span] = dq.astype(BF16)
        dkv_ref[:, span] = dk.astype(BF16)
        dkv_ref[:, far] = dv.astype(BF16)


def attend(query_place, key_place, q, kv):
    rows, width = q.shape
    return pl.pallas_call(
        attend_kernel,
        out_shape=(
            jax.ShapeDtypeStruct((rows, width), F32),
            jax.ShapeDtypeStruct((rows, LANES), F32),
        ),
        compiler_params=pltpu.CompilerParams(vmem_limit_bytes=48 * 2**20),
    )(query_place, key_place, q, kv)


def attend_back(query_place, key_place, q, kv, attended, grad, logs):
    return pl.pallas_call(
        attend_back_kernel,
        out_shape=(
            jax.ShapeDtypeStruct(q.shape, BF16),
            jax.ShapeDtypeStruct(kv.shape, BF16),
        ),
        compiler_params=pltpu.CompilerParams(vmem_limit_bytes=48 * 2**20),
    )(query_place, key_place, q, kv, attended, grad, logs)


def shards(
    inputs,
    cotangent,
    block_order,
    norm1_gain,
    norm1_shift,
    w_qkv,
    qv_bias,
    w_out,
    out_bias,
    norm2_gain,
    norm2_shift,
    w_fc,
    fc_bias,
    w_proj,
    proj_bias,
):
    rows, width = inputs.shape[1:]
    positions = lax.axis_size("ctx")
    spread = lax.axis_size("fsdp")
    place = lax.axis_index("ctx")
    core = place % 2
    pairs = [[2 * i, 2 * i + 1] for i in range(positions // 2)]
    lines = [list(range(j, positions, 2)) for j in range(2)]
    shard = width // spread

    def half_of(weight):
        half = weight.shape[1] // 2
        return lax.dynamic_slice_in_dim(weight, core * half, half, 1)

    def gather(weight):
        across = lax.all_gather(weight, "fsdp", axis=0, tiled=True)
        return lax.all_gather(across, "ctx", axis=0, tiled=False, axis_index_groups=pairs)

    def reduce(halves):
        mine = lax.psum_scatter(
            halves, "ctx", scatter_dimension=0, tiled=False, axis_index_groups=pairs
        )
        mine = lax.psum_scatter(mine, "fsdp", scatter_dimension=0, tiled=True)
        mine = lax.psum(mine, "ctx", axis_index_groups=lines)
        return lax.all_gather(mine, "ctx", axis=0, tiled=False, axis_index_groups=pairs)

    def join(halves, begin, end):
        return jnp.concatenate([halves[0][:, begin:end], halves[1][:, begin:end]], axis=1)

    small = jnp.concatenate(
        [
            norm1_gain[None],
            norm1_shift[None],
            qv_bias,
            out_bias[None],
            norm2_gain[None],
            norm2_shift[None],
            proj_bias[None],
            fc_bias.reshape(-1, shard),
        ]
    )
    small = lax.all_gather(small, "fsdp", axis=0).astype(F32)
    vectors = jnp.moveaxis(small[:, :8], 0, 1).reshape(8, width)
    gain_one, shift_one, q_bias, v_bias, out_shift, gain_two, shift_two, proj_shift = vectors
    fc_shift = small[:, 8:].reshape(-1)

    qkv_w = gather(half_of(w_qkv))
    wide = gather(jnp.concatenate([half_of(w_out), half_of(w_fc)], axis=1))
    proj_w = gather(half_of(w_proj))
    out_half = width // 2
    qkv_full = join(qkv_w, 0, qkv_w.shape[2])
    out_full = join(wide, 0, out_half)
    fc_full = join(wide, out_half, wide.shape[2])
    proj_full = join(proj_w, 0, out_half)

    tokens = inputs[0].astype(F32)
    unit_one, inverse_one = normalise(tokens)
    normed_one = (unit_one * gain_one + shift_one).astype(BF16)
    qkv_shift = jnp.concatenate([q_bias, jnp.zeros_like(q_bias), v_bias])
    qkv = (dot(normed_one, qkv_full) + qkv_shift).astype(BF16)
    q = qkv[:, :width]
    kv = lax.all_gather(qkv[:, width:], "ctx", axis=0, tiled=True)
    block_rows = kv.shape[0] // block_order.shape[0]
    query_place = block_places(block_order, place * rows, rows, block_rows)[:, None]
    key_place = block_places(block_order, jnp.int32(0), kv.shape[0], block_rows)[None]
    attended, logs = attend(query_place, key_place, q, kv)
    attended_low = attended.astype(BF16)
    middle = tokens + dot(attended_low, out_full) + out_shift
    unit_two, inverse_two = normalise(middle)
    normed_two = (unit_two * gain_two + shift_two).astype(BF16)
    hidden = dot(normed_two, fc_full) + fc_shift
    activated, slope = gelu_pair(hidden)
    activated = activated.astype(BF16)
    output = middle + dot(activated, proj_full) + proj_shift

    grad_output = cotangent[0]

    def split(left, right):
        half = right.shape[1] // 2
        return jnp.stack(
            [dot_rows(left, right[:, :half]), dot_rows(left, right[:, half:])]
        ).astype(BF16)

    proj_grad = reduce(split(activated, grad_output))
    grad_hidden = (dot_lanes(grad_output, proj_full) * slope).astype(BF16)
    fc_grad = split(normed_two, grad_hidden)
    grad_normed_two = dot_lanes(grad_hidden, fc_full)
    grad_middle = grad_output.astype(F32) + norm_backward(
        grad_normed_two, gain_two, unit_two, inverse_two
    )
    grad_branch = grad_middle.astype(BF16)
    out_grad = split(attended_low, grad_branch)
    wide_grad = reduce(jnp.concatenate([out_grad, fc_grad], axis=2))
    grad_attended = dot_lanes(grad_branch, out_full).astype(BF16)
    dq, dkv = attend_back(query_place, key_place, q, kv, attended, grad_attended, logs)
    dkv = lax.psum_scatter(dkv, "ctx", scatter_dimension=0, tiled=True)
    grad_qkv = jnp.concatenate([dq, dkv], axis=1)
    qkv_grad = reduce(split(normed_one, grad_qkv))
    grad_normed_one = dot_lanes(grad_qkv, qkv_full)
    grad_tokens = grad_middle + norm_backward(grad_normed_one, gain_one, unit_one, inverse_one)

    def total(values):
        return jnp.sum(values, axis=0, dtype=F32)

    columns = total(grad_qkv)
    small_grad = jnp.stack(
        [
            total(grad_normed_one * unit_one),
            total(grad_normed_one),
            columns[:width],
            columns[2 * width :],
            total(grad_branch),
            total(grad_normed_two * unit_two),
            total(grad_normed_two),
            total(grad_output),
        ]
    )
    small_grad = jnp.moveaxis(small_grad.reshape(8, spread, shard), 1, 0)
    small_grad = jnp.concatenate(
        [small_grad, total(grad_hidden).reshape(spread, -1, shard)], axis=1
    )
    small_grad = lax.psum_scatter(small_grad, "fsdp", scatter_dimension=0, tiled=False)
    small_grad = lax.psum(small_grad, "ctx")

    def whole(halves, begin, end):
        return join(halves, begin, end).astype(F32)

    return (
        output[None].astype(BF16),
        grad_tokens[None].astype(BF16),
        small_grad[0],
        small_grad[1],
        whole(qkv_grad, 0, qkv_grad.shape[2]),
        small_grad[2:4],
        whole(wide_grad, 0, out_half),
        small_grad[4],
        small_grad[5],
        small_grad[6],
        whole(wide_grad, out_half, wide_grad.shape[2]),
        small_grad[8:].reshape(-1),
        whole(proj_grad, 0, out_half),
        small_grad[7],
    )


def solution(mesh):
    in_specs = (
        P("fsdp", "ctx", None),
        P("fsdp", "ctx", None),
        P(),
        P("fsdp"),
        P("fsdp"),
        P("fsdp", None),
        P(None, "fsdp"),
        P("fsdp", None),
        P("fsdp"),
        P("fsdp"),
        P("fsdp"),
        P("fsdp", None),
        P("fsdp"),
        P("fsdp", None),
        P("fsdp"),
    )
    out_specs = (
        P("fsdp", "ctx", None),
        P("fsdp", "ctx", None),
        P("fsdp"),
        P("fsdp"),
        P("fsdp", None),
        P(None, "fsdp"),
        P("fsdp", None),
        P("fsdp"),
        P("fsdp"),
        P("fsdp"),
        P("fsdp", None),
        P("fsdp"),
        P("fsdp", None),
        P("fsdp"),
    )
    return jax.shard_map(shards, mesh=mesh, in_specs=in_specs, out_specs=out_specs, check_vma=False)
```

```python
from functools import partial

import jax
import jax.numpy as jnp
from jax import lax
from jax.experimental import pallas as pl
from jax.experimental.pallas import tpu as pltpu
from jax.sharding import PartitionSpec as P

HEADS = 12
EPS = 1e-05
LOWEST = -1e30
LANES = 128
F32 = jnp.float32
BF16 = jnp.bfloat16
ROW_DOT = (((0,), (0,)), ((), ()))
LANE_DOT = (((1,), (1,)), ((), ()))


def dot(left, right):
    return jnp.dot(left, right, preferred_element_type=F32)


def dot_rows(left, right):
    return lax.dot_general(left, right, ROW_DOT, preferred_element_type=F32)


def dot_lanes(left, right):
    return lax.dot_general(left, right, LANE_DOT, preferred_element_type=F32)


def normalise(values):
    centred = values - jnp.mean(values, axis=-1, keepdims=True)
    spread = jnp.mean(centred * centred, axis=-1, keepdims=True)
    inverse = lax.rsqrt(spread + EPS)
    return centred * inverse, inverse


def norm_backward(incoming, gain, unit, inverse):
    scaled = incoming * gain
    first = jnp.mean(scaled, axis=-1, keepdims=True)
    second = jnp.mean(scaled * unit, axis=-1, keepdims=True)
    return inverse * (scaled - first - unit * second)


def gelu_pair(values):
    inner = 0.7978845608028654 * (values + 0.044715 * values * values * values)
    bent = jnp.tanh(inner)
    slope = 0.7978845608028654 * (1.0 + 0.134145 * values * values)
    value = 0.5 * values * (1.0 + bent)
    derivative = 0.5 * (1.0 + bent) + 0.5 * values * (1.0 - bent * bent) * slope
    return value, derivative


def block_places(block_order, first_row, row_count, block_rows):
    row_index = first_row + jnp.arange(row_count, dtype=jnp.int32)
    which_block = row_index // block_rows
    table = jnp.arange(block_order.shape[0], dtype=jnp.int32)
    picked = jnp.sum(
        jnp.where(which_block[:, None] == table[None, :], block_order[None, :], 0), axis=1
    )
    return picked * block_rows + row_index % block_rows


def attend_kernel(query_place, key_place, q_ref, kv_ref, out_ref, log_ref):
    rows, width = q_ref.shape
    head_dim = width // HEADS
    per_group = LANES // head_dim
    visible = key_place[...] <= query_place[...]
    lane = lax.broadcasted_iota(jnp.int32, (rows, LANES), 1)
    logs = jnp.zeros((rows, LANES), F32)
    for group in range(width // LANES):
        span = pl.ds(group * LANES, LANES)
        q = q_ref[:, span] * (head_dim**-0.5)
        k = kv_ref[:, span]
        v = kv_ref[:, pl.ds(width + group * LANES, LANES)]
        out = jnp.zeros((rows, LANES), F32)
        for part in range(per_group):
            own = lane // head_dim == part
            scores = dot_lanes(jnp.where(own, q, jnp.zeros_like(q)), k)
            scores = jnp.where(visible, scores, LOWEST)
            high = jnp.max(scores, axis=1, keepdims=True)
            shares = jnp.exp(scores - high)
            total = jnp.sum(shares, axis=1, keepdims=True)
            out = jnp.where(own, dot(shares.astype(BF16), v) / total, out)
            logs = jnp.where(lane == group * per_group + part, high + jnp.log(total), logs)
        out_ref[:, span] = out
    log_ref[...] = logs


def attend_back_kernel(
    query_place, key_place, q_ref, kv_ref, att_ref, grad_ref, log_ref, dq_ref, dkv_ref
):
    rows, width = q_ref.shape
    head_dim = width // HEADS
    per_group = LANES // head_dim
    scale = head_dim**-0.5
    visible = key_place[...] <= query_place[...]
    lane = lax.broadcasted_iota(jnp.int32, (rows, LANES), 1)
    for group in range(width // LANES):
        span = pl.ds(group * LANES, LANES)
        far = pl.ds(width + group * LANES, LANES)
        q = q_ref[:, span] * scale
        k = kv_ref[:, span]
        v = kv_ref[:, far]
        grad = grad_ref[:, span]
        product = grad.astype(F32) * att_ref[:, span]
        dq = jnp.zeros((rows, LANES), F32)
        dk = jnp.zeros((k.shape[0], LANES), F32)
        dv = jnp.zeros((k.shape[0], LANES), F32)
        for part in range(per_group):
            own = lane // head_dim == part
            own_q = jnp.where(own, q, jnp.zeros_like(q))
            own_grad = jnp.where(own, grad, jnp.zeros_like(grad))
            delta = jnp.sum(jnp.where(own, product, 0.0), axis=1, keepdims=True)
            log = jnp.sum(
                jnp.where(lane == group * per_group + part, log_ref[...], 0.0),
                axis=1,
                keepdims=True,
            )
            scores = jnp.where(visible, dot_lanes(own_q, k), LOWEST)
            shares = jnp.exp(scores - log)
            dv = dv + dot_rows(shares.astype(BF16), own_grad)
            change = (shares * (dot_lanes(own_grad, v) - delta)).astype(BF16)
            dq = jnp.where(own, dot(change, k) * scale, dq)
            dk = dk + dot_rows(change, own_q)
        dq_ref[:, span] = dq.astype(BF16)
        dkv_ref[:, span] = dk.astype(BF16)
        dkv_ref[:, far] = dv.astype(BF16)


def attend(query_place, key_place, q, kv):
    rows, width = q.shape
    return pl.pallas_call(
        attend_kernel,
        out_shape=(
            jax.ShapeDtypeStruct((rows, width), F32),
            jax.ShapeDtypeStruct((rows, LANES), F32),
        ),
        compiler_params=pltpu.CompilerParams(vmem_limit_bytes=48 * 2**20),
    )(query_place, key_place, q, kv)


def attend_back(query_place, key_place, q, kv, attended, grad, logs):
    return pl.pallas_call(
        attend_back_kernel,
        out_shape=(
            jax.ShapeDtypeStruct(q.shape, BF16),
            jax.ShapeDtypeStruct(kv.shape, BF16),
        ),
        compiler_params=pltpu.CompilerParams(vmem_limit_bytes=48 * 2**20),
    )(query_place, key_place, q, kv, attended, grad, logs)

MESH = pl.DeviceIdType.MESH
GATHER_ID = 0
REDUCE_ID = 1


def ring_order(fsdp, depth):
    across = fsdp // depth
    order = []
    for z in range(depth):
        columns = list(range(1, across))
        order += [z * across + y for y in (columns if z % 2 == 0 else columns[::-1])]
    return order + [z * across for z in range(depth - 1, -1, -1)]


def pick(table, index):
    found = jnp.int32(table[0])
    for at in range(1, len(table)):
        found = jnp.where(index == at, jnp.int32(table[at]), found)
    return found


def ring_blocks(order, position):
    size = len(order)
    return [pick(order, lax.rem(position + shift, size)) for shift in range(size)]


def remote(source, target, send, receive, device):
    return pltpu.make_async_remote_copy(
        src_ref=source,
        dst_ref=target,
        send_sem=send,
        recv_sem=receive,
        device_id=device,
        device_id_type=MESH,
    )


def greet(devices):
    barrier = pltpu.get_barrier_semaphore()
    for device in devices:
        pl.semaphore_signal(barrier, inc=1, device_id=device, device_id_type=MESH)
    pl.semaphore_wait(barrier, len(devices))


def gather_kernel(order, count, *refs):
    ins, outs = refs[:count], refs[count : 2 * count]
    send, receive, pair_send, pair_receive, local = refs[2 * count :]
    size = len(order)
    me, ctx = lax.axis_index("fsdp"), lax.axis_index("ctx")
    core = lax.rem(ctx, 2)
    sibling = (me, ctx + 1 - 2 * core)
    inverse = [order.index(at) for at in range(size)]
    block = ring_blocks(order, pick(inverse, me))
    following, preceding = (block[1], ctx), (block[size - 1], ctx)
    greet([following, preceding, sibling])
    started = []
    for a in range(count):
        copy = pltpu.make_async_copy(ins[a].at[core], outs[a].at[me, core], local.at[a])
        copy.start()
        started.append(copy)
    pending = []
    hops = [(size // 2, size - 1 - size // 2), (size - 1 - size // 2, size // 2)]
    for step in range(size // 2 + 1):
        for a in range(count):
            for way in range(2):
                total = hops[a % 2][way]
                shift = (size - step) % size if way == 0 else step
                at = block[shift]
                source = outs[a].at[at, core] if step else ins[a].at[core]
                if 0 < step <= total:
                    remote(
                        source, source, send.at[a, way, step - 1],
                        receive.at[a, way, step - 1], following,
                    ).wait_recv()
                if step < total:
                    copy = remote(
                        source, outs[a].at[at, core], send.at[a, way, step],
                        receive.at[a, way, step], following if way == 0 else preceding,
                    )
                    copy.start()
                    pending.append(copy)
                if 0 < step <= total or (step == 0 and way == 0):
                    copy = remote(
                        source, outs[a].at[at, core], pair_send.at[a, shift],
                        pair_receive.at[a, shift], sibling,
                    )
                    copy.start()
                    pending.append(copy)
    for a in range(count):
        for shift in range(size):
            target = outs[a].at[block[shift], 1 - core]
            remote(
                target, target, pair_send.at[a, shift], pair_receive.at[a, shift], sibling
            ).wait_recv()
    for copy in pending:
        copy.wait_send()
    for copy in started:
        copy.wait()


def gather_all(shards, order):
    count, size = len(shards), len(order)
    dma = pltpu.SemaphoreType.DMA
    return pl.pallas_call(
        partial(gather_kernel, order, count),
        out_shape=[jax.ShapeDtypeStruct((size,) + s.shape, s.dtype) for s in shards],
        in_specs=[pl.BlockSpec(memory_space=pl.ANY)] * count,
        out_specs=[pl.BlockSpec(memory_space=pl.ANY)] * count,
        scratch_shapes=[
            dma((count, 2, size // 2)),
            dma((count, 2, size // 2)),
            dma((count, size)),
            dma((count, size)),
            dma((count,)),
        ],
        compiler_params=pltpu.CompilerParams(collective_id=GATHER_ID, has_side_effects=True),
    )(*shards)


def reduce_kernel(order, lines, count, *refs):
    ins, outs = refs[:count], refs[count : 2 * count]
    pairs = refs[2 * count : 3 * count]
    slots = refs[3 * count : 4 * count]
    crossed = refs[4 * count : 5 * count]
    ring_send, ring_receive, pair_send, pair_receive = refs[5 * count : 5 * count + 4]
    line_send, line_receive, last_send, last_receive = refs[5 * count + 4 :]
    size = len(order)
    me, ctx = lax.axis_index("fsdp"), lax.axis_index("ctx")
    core = lax.rem(ctx, 2)
    line = ctx // 2
    sibling = (me, ctx + 1 - 2 * core)
    inverse = [order.index(at) for at in range(size)]
    block = ring_blocks(order, pick(inverse, me))
    ways = [(block[1], ctx), (block[size - 1], ctx)]
    peers = [(me, lax.rem(line + k, lines) * 2 + core) for k in range(1, lines)]
    greet(ways + [sibling] + peers)
    pending = []

    def shift_of(way, step):
        return (size - 1 - step) % size if way == 0 else (1 + step) % size

    ready = []
    for step in range(size):
        for way in range(2):
            shift = shift_of(way, step)
            if shift not in ready:
                ready.append(shift)
                for a in range(count):
                    copy = remote(
                        ins[a].at[block[shift], 1 - core], pairs[a].at[block[shift]],
                        pair_send.at[a, shift], pair_receive.at[a, shift], sibling,
                    )
                    copy.start()
                    pending.append(copy)
    waited = []

    def arrive(shift):
        if shift not in waited:
            waited.append(shift)
            for a in range(count):
                target = pairs[a].at[block[shift]]
                remote(
                    target, target, pair_send.at[a, shift], pair_receive.at[a, shift], sibling
                ).wait_recv()

    for step in range(size):
        for way in range(2):
            shift = shift_of(way, step)
            arrive(shift)
            at = block[shift]
            for a in range(count):
                half = ins[a].shape[3] // 2
                span = pl.ds(way * half, half)
                value = ins[a][at, core, :, span].astype(F32) + pairs[a][at, :, span].astype(F32)
                if step:
                    slot = slots[a].at[way, step - 1]
                    remote(
                        slot, slot, ring_send.at[a, way, step - 1],
                        ring_receive.at[a, way, step - 1], ways[way],
                    ).wait_recv()
                    value = value + slot[...].astype(F32)
                if step < size - 1:
                    held = slots[a].at[way, step - 1 if step else size - 1]
                    held[...] = value.astype(BF16)
                    copy = remote(
                        held, slots[a].at[way, step], ring_send.at[a, way, step],
                        ring_receive.at[a, way, step], ways[way],
                    )
                    copy.start()
                    pending.append(copy)
                else:
                    crossed[a][line, :, span] = value.astype(BF16)
    for a in range(count):
        for k in range(1, lines):
            copy = remote(
                crossed[a].at[line], crossed[a].at[line], line_send.at[a, k - 1],
                line_receive.at[a, k - 1], peers[k - 1],
            )
            copy.start()
            pending.append(copy)
    for a in range(count):
        for k in range(1, lines):
            target = crossed[a].at[lax.rem(line + lines - k, lines)]
            remote(
                target, target, line_send.at[a, k - 1], line_receive.at[a, k - 1], peers[k - 1]
            ).wait_recv()
        value = crossed[a][0].astype(F32)
        for k in range(1, lines):
            value = value + crossed[a][k].astype(F32)
        outs[a][core] = value.astype(BF16)
        copy = remote(
            outs[a].at[core], outs[a].at[core], last_send.at[a], last_receive.at[a], sibling
        )
        copy.start()
        pending.append(copy)
    for a in range(count):
        target = outs[a].at[1 - core]
        remote(target, target, last_send.at[a], last_receive.at[a], sibling).wait_recv()
    for copy in pending:
        copy.wait_send()


def reduce_all(grads, order, lines):
    count, size = len(grads), len(order)
    dma = pltpu.SemaphoreType.DMA
    vmem = pl.BlockSpec(memory_space=pltpu.VMEM)
    scratch = [pltpu.VMEM((size,) + g.shape[2:], BF16) for g in grads]
    scratch += [pltpu.VMEM((2, size, g.shape[2], g.shape[3] // 2), BF16) for g in grads]
    scratch += [pltpu.VMEM((lines,) + g.shape[2:], BF16) for g in grads]
    scratch += [dma((count, 2, size - 1)), dma((count, 2, size - 1))]
    scratch += [dma((count, size)), dma((count, size))]
    scratch += [dma((count, max(lines - 1, 1))), dma((count, max(lines - 1, 1)))]
    scratch += [dma((count,)), dma((count,))]
    return pl.pallas_call(
        partial(reduce_kernel, order, lines, count),
        out_shape=[jax.ShapeDtypeStruct(g.shape[1:], BF16) for g in grads],
        in_specs=[vmem] * count,
        out_specs=[vmem] * count,
        scratch_shapes=scratch,
        compiler_params=pltpu.CompilerParams(
            collective_id=REDUCE_ID, has_side_effects=True, vmem_limit_bytes=56 * 2**20
        ),
    )(*grads)


def round_up(value, unit):
    return -(-value // unit) * unit


def pad_to(array, shape):
    return jnp.pad(array, [(0, new - old) for old, new in zip(array.shape, shape)])


def shards(
    inputs,
    cotangent,
    block_order,
    norm1_gain,
    norm1_shift,
    w_qkv,
    qv_bias,
    w_out,
    out_bias,
    norm2_gain,
    norm2_shift,
    w_fc,
    fc_bias,
    w_proj,
    proj_bias,
):
    rows, width = inputs.shape[1:]
    positions = lax.axis_size("ctx")
    spread = lax.axis_size("fsdp")
    place = lax.axis_index("ctx")
    lines = positions // 2
    order = ring_order(spread, spread // lines if spread % lines == 0 else spread // 2)
    shard = width // spread
    sixteen = 16

    def two(weight):
        part = weight.shape[0] // 2
        weight = weight.reshape(2, part, weight.shape[1])
        return pad_to(weight, (2, round_up(part, sixteen), weight.shape[2]))

    def full(gathered, weight):
        part = weight.shape[0] // 2
        return gathered[:, :, :part].reshape(-1, weight.shape[1])

    def spread_out(grad):
        part = grad.shape[0] // spread // 2
        grad = grad.astype(BF16).reshape(spread, 2, part, grad.shape[1])
        return pad_to(grad, (spread, 2, round_up(part, sixteen), grad.shape[3]))

    def own(reduced, weight):
        part = weight.shape[0] // 2
        return reduced[:, :part].reshape(weight.shape).astype(F32)

    small = jnp.concatenate(
        [
            norm1_gain[None],
            norm1_shift[None],
            qv_bias,
            out_bias[None],
            norm2_gain[None],
            norm2_shift[None],
            proj_bias[None],
            fc_bias.reshape(-1, shard),
        ]
    )
    small_rows = small.shape[0]
    small = pad_to(small, (2 * sixteen, round_up(shard, LANES))).reshape(2, sixteen, -1)
    qkv_full, fc_full, out_full, proj_full, small = gather_all(
        [two(w_qkv), two(w_fc), two(w_out), two(w_proj), small], order
    )
    qkv_full = full(qkv_full, w_qkv)
    fc_full = full(fc_full, w_fc)
    out_full = full(out_full, w_out)
    proj_full = full(proj_full, w_proj)
    small = small.reshape(spread, 2 * sixteen, -1)[:, :small_rows, :shard].astype(F32)
    vectors = jnp.moveaxis(small[:, :8], 0, 1).reshape(8, width)
    gain_one, shift_one, q_bias, v_bias, out_shift, gain_two, shift_two, proj_shift = vectors
    fc_shift = small[:, 8:].reshape(-1)

    tokens = inputs[0].astype(F32)
    unit_one, inverse_one = normalise(tokens)
    normed_one = (unit_one * gain_one + shift_one).astype(BF16)
    qkv_shift = jnp.concatenate([q_bias, jnp.zeros_like(q_bias), v_bias])
    qkv = (dot(normed_one, qkv_full) + qkv_shift).astype(BF16)
    q = qkv[:, :width]
    kv = lax.all_gather(qkv[:, width:], "ctx", axis=0, tiled=True)
    block_rows = kv.shape[0] // block_order.shape[0]
    query_place = block_places(block_order, place * rows, rows, block_rows)[:, None]
    key_place = block_places(block_order, jnp.int32(0), kv.shape[0], block_rows)[None]
    attended, logs = attend(query_place, key_place, q, kv)
    attended_low = attended.astype(BF16)
    middle = tokens + dot(attended_low, out_full) + out_shift
    unit_two, inverse_two = normalise(middle)
    normed_two = (unit_two * gain_two + shift_two).astype(BF16)
    hidden = dot(normed_two, fc_full) + fc_shift
    activated, slope = gelu_pair(hidden)
    activated = activated.astype(BF16)
    output = middle + dot(activated, proj_full) + proj_shift

    grad_output = cotangent[0]

    proj_grad = dot_rows(activated, grad_output)
    grad_hidden = (dot_lanes(grad_output, proj_full) * slope).astype(BF16)
    fc_grad = dot_rows(normed_two, grad_hidden)
    grad_normed_two = dot_lanes(grad_hidden, fc_full)
    grad_middle = grad_output.astype(F32) + norm_backward(
        grad_normed_two, gain_two, unit_two, inverse_two
    )
    grad_branch = grad_middle.astype(BF16)
    out_grad = dot_rows(attended_low, grad_branch)
    grad_attended = dot_lanes(grad_branch, out_full).astype(BF16)
    dq, dkv = attend_back(query_place, key_place, q, kv, attended, grad_attended, logs)
    dkv = lax.psum_scatter(dkv, "ctx", scatter_dimension=0, tiled=True)
    grad_qkv = jnp.concatenate([dq, dkv], axis=1)
    qkv_grad = dot_rows(normed_one, grad_qkv)
    grad_normed_one = dot_lanes(grad_qkv, qkv_full)
    grad_tokens = grad_middle + norm_backward(grad_normed_one, gain_one, unit_one, inverse_one)

    def total(values):
        return jnp.sum(values, axis=0, dtype=F32)

    columns = total(grad_qkv)
    small_grad = jnp.stack(
        [
            total(grad_normed_one * unit_one),
            total(grad_normed_one),
            columns[:width],
            columns[2 * width :],
            total(grad_branch),
            total(grad_normed_two * unit_two),
            total(grad_normed_two),
            total(grad_output),
        ]
    )
    small_grad = jnp.moveaxis(small_grad.reshape(8, spread, shard), 1, 0)
    small_grad = jnp.concatenate(
        [small_grad, total(grad_hidden).reshape(spread, -1, shard)], axis=1
    )
    small_grad = pad_to(
        small_grad, (spread, 2 * sixteen, round_up(shard, 2 * LANES))
    ).reshape(spread, 2, sixteen, -1)
    qkv_grad, fc_grad, out_grad, proj_grad, small_grad = reduce_all(
        [
            spread_out(qkv_grad),
            spread_out(fc_grad),
            spread_out(out_grad),
            spread_out(proj_grad),
            small_grad.astype(BF16),
        ],
        order,
        lines,
    )
    small_grad = small_grad.reshape(2 * sixteen, -1)[:small_rows, :shard].astype(F32)

    return (
        output[None].astype(BF16),
        grad_tokens[None].astype(BF16),
        small_grad[0],
        small_grad[1],
        own(qkv_grad, w_qkv),
        small_grad[2:4],
        own(out_grad, w_out),
        small_grad[4],
        small_grad[5],
        small_grad[6],
        own(fc_grad, w_fc),
        small_grad[8:].reshape(-1),
        own(proj_grad, w_proj),
        small_grad[7],
    )


def solution(mesh):
    in_specs = (
        P("fsdp", "ctx", None),
        P("fsdp", "ctx", None),
        P(),
        P("fsdp"),
        P("fsdp"),
        P("fsdp", None),
        P(None, "fsdp"),
        P("fsdp", None),
        P("fsdp"),
        P("fsdp"),
        P("fsdp"),
        P("fsdp", None),
        P("fsdp"),
        P("fsdp", None),
        P("fsdp"),
    )
    out_specs = (
        P("fsdp", "ctx", None),
        P("fsdp", "ctx", None),
        P("fsdp"),
        P("fsdp"),
        P("fsdp", None),
        P(None, "fsdp"),
        P("fsdp", None),
        P("fsdp"),
        P("fsdp"),
        P("fsdp"),
        P("fsdp", None),
        P("fsdp"),
        P("fsdp", None),
        P("fsdp"),
    )
    return jax.shard_map(shards, mesh=mesh, in_specs=in_specs, out_specs=out_specs, check_vma=False)
```

```python
from functools import partial

import jax
import jax.numpy as jnp
from jax import lax
from jax.experimental import pallas as pl
from jax.experimental.pallas import tpu as pltpu
from jax.sharding import PartitionSpec as P

HEADS = 12
EPS = 1e-05
LOWEST = -1e30
LANES = 128
F32 = jnp.float32
BF16 = jnp.bfloat16
ROW_DOT = (((0,), (0,)), ((), ()))
LANE_DOT = (((1,), (1,)), ((), ()))


def dot(left, right):
    return jnp.dot(left, right, preferred_element_type=F32)


def dot_rows(left, right):
    return lax.dot_general(left, right, ROW_DOT, preferred_element_type=F32)


def dot_lanes(left, right):
    return lax.dot_general(left, right, LANE_DOT, preferred_element_type=F32)


def normalise(values):
    centred = values - jnp.mean(values, axis=-1, keepdims=True)
    spread = jnp.mean(centred * centred, axis=-1, keepdims=True)
    inverse = lax.rsqrt(spread + EPS)
    return centred * inverse, inverse


def norm_backward(incoming, gain, unit, inverse):
    scaled = incoming * gain
    first = jnp.mean(scaled, axis=-1, keepdims=True)
    second = jnp.mean(scaled * unit, axis=-1, keepdims=True)
    return inverse * (scaled - first - unit * second)


def gelu_pair(values):
    inner = 0.7978845608028654 * (values + 0.044715 * values * values * values)
    bent = jnp.tanh(inner)
    slope = 0.7978845608028654 * (1.0 + 0.134145 * values * values)
    value = 0.5 * values * (1.0 + bent)
    derivative = 0.5 * (1.0 + bent) + 0.5 * values * (1.0 - bent * bent) * slope
    return value, derivative


def block_places(block_order, first_row, row_count, block_rows):
    row_index = first_row + jnp.arange(row_count, dtype=jnp.int32)
    which_block = row_index // block_rows
    table = jnp.arange(block_order.shape[0], dtype=jnp.int32)
    picked = jnp.sum(
        jnp.where(which_block[:, None] == table[None, :], block_order[None, :], 0), axis=1
    )
    return picked * block_rows + row_index % block_rows


def attend_part(query_place, key_place, q_ref, kv_ref, out_ref, log_ref):
    rows, width = q_ref.shape
    head_dim = width // HEADS
    per_group = LANES // head_dim
    visible = key_place[...] <= query_place[...]
    lane = lax.broadcasted_iota(jnp.int32, (rows, LANES), 1)
    logs = jnp.zeros((rows, LANES), F32)
    for group in range(width // LANES):
        span = pl.ds(group * LANES, LANES)
        q = q_ref[:, span] * (head_dim**-0.5)
        k = kv_ref[:, :, span].reshape(-1, LANES)
        v = kv_ref[:, :, pl.ds(width + group * LANES, LANES)].reshape(-1, LANES)
        out = jnp.zeros((rows, LANES), F32)
        for part in range(per_group):
            own = lane // head_dim == part
            scores = dot_lanes(jnp.where(own, q, jnp.zeros_like(q)), k)
            scores = jnp.where(visible, scores, LOWEST)
            high = jnp.max(scores, axis=1, keepdims=True)
            shares = jnp.exp(scores - high)
            total = jnp.sum(shares, axis=1, keepdims=True)
            out = jnp.where(own, dot(shares.astype(BF16), v) / total, out)
            logs = jnp.where(lane == group * per_group + part, high + jnp.log(total), logs)
        out_ref[:, span] = out
    log_ref[...] = logs


def attend_back_part(
    groups, query_place, key_place, q_ref, kv_ref, att_ref, grad_ref, log_ref, dq_ref, dkv_ref
):
    rows, width = q_ref.shape
    head_dim = width // HEADS
    per_group = LANES // head_dim
    scale = head_dim**-0.5
    visible = key_place[...] <= query_place[...]
    lane = lax.broadcasted_iota(jnp.int32, (rows, LANES), 1)
    for group in groups:
        span = pl.ds(group * LANES, LANES)
        far = pl.ds(width + group * LANES, LANES)
        q = q_ref[:, span] * scale
        k = kv_ref[:, :, span].reshape(-1, LANES)
        v = kv_ref[:, :, far].reshape(-1, LANES)
        grad = grad_ref[:, span]
        product = grad.astype(F32) * att_ref[:, span]
        dq = jnp.zeros((rows, LANES), F32)
        dk = jnp.zeros((k.shape[0], LANES), F32)
        dv = jnp.zeros((k.shape[0], LANES), F32)
        for part in range(per_group):
            own = lane // head_dim == part
            own_q = jnp.where(own, q, jnp.zeros_like(q))
            own_grad = jnp.where(own, grad, jnp.zeros_like(grad))
            delta = jnp.sum(jnp.where(own, product, 0.0), axis=1, keepdims=True)
            log = jnp.sum(
                jnp.where(lane == group * per_group + part, log_ref[...], 0.0),
                axis=1,
                keepdims=True,
            )
            scores = jnp.where(visible, dot_lanes(own_q, k), LOWEST)
            shares = jnp.exp(scores - log)
            dv = dv + dot_rows(shares.astype(BF16), own_grad)
            change = (shares * (dot_lanes(own_grad, v) - delta)).astype(BF16)
            dq = jnp.where(own, dot(change, k) * scale, dq)
            dk = dk + dot_rows(change, own_q)
        dq_ref[:, span] = dq.astype(BF16)
        shape = (kv_ref.shape[0], rows, LANES)
        dkv_ref[:, :, span] = dk.astype(BF16).reshape(shape)
        dkv_ref[:, :, far] = dv.astype(BF16).reshape(shape)


MESH = pl.DeviceIdType.MESH


def ring_order(fsdp, depth):
    across = fsdp // depth
    order = []
    for z in range(depth):
        columns = list(range(1, across))
        order += [z * across + y for y in (columns if z % 2 == 0 else columns[::-1])]
    return order + [z * across for z in range(depth - 1, -1, -1)]


def pick(table, index):
    found = jnp.int32(table[0])
    for at in range(1, len(table)):
        found = jnp.where(index == at, jnp.int32(table[at]), found)
    return found


def ring_blocks(order, position):
    size = len(order)
    return [pick(order, lax.rem(position + shift, size)) for shift in range(size)]


def remote(source, target, send, receive, device):
    return pltpu.make_async_remote_copy(
        src_ref=source,
        dst_ref=target,
        send_sem=send,
        recv_sem=receive,
        device_id=device,
        device_id_type=MESH,
    )


def greet(devices):
    barrier = pltpu.get_barrier_semaphore()
    for device in devices:
        pl.semaphore_signal(barrier, inc=1, device_id=device, device_id_type=MESH)
    pl.semaphore_wait(barrier, len(devices))


def attend_hooks(lines, ctx, sibling, peers, pending, ins, outs, sems):
    query_place, key_place, q_ref, own_ref = ins
    kv_ref, out_ref, log_ref = outs
    send, receive, pair_send, pair_receive = sems
    core, line = lax.rem(ctx, 2), ctx // 2

    def to_sibling(source, at, slot):
        copy = remote(source, kv_ref.at[at], pair_send.at[slot], pair_receive.at[slot], sibling)
        copy.start()
        pending.append(copy)

    def begin():
        for k in range(1, lines):
            copy = remote(
                own_ref, kv_ref.at[ctx], send.at[k - 1], receive.at[k - 1], peers[k - 1]
            )
            copy.start()
            pending.append(copy)
        to_sibling(own_ref, ctx, 0)
        kv_ref[ctx] = own_ref[...]

    def relay():
        for k in range(1, lines):
            at = lax.rem(line + lines - k, lines) * 2 + core
            target = kv_ref.at[at]
            remote(target, target, send.at[k - 1], receive.at[k - 1], peers[k - 1]).wait_recv()
            to_sibling(target, at, k)

    def compute():
        for k in range(lines):
            target = kv_ref.at[lax.rem(line + lines - k, lines) * 2 + 1 - core]
            remote(target, target, pair_send.at[k], pair_receive.at[k], sibling).wait_recv()
        attend_part(query_place, key_place, q_ref, kv_ref, out_ref, log_ref)

    return {0: begin, 1: relay, 2: compute}


def gather_kernel(order, lines, count, extra, *refs):
    ins, side_in = refs[:count], refs[count : count + extra[0]]
    refs = refs[count + extra[0] :]
    outs, side_out = refs[:count], refs[count : count + extra[1]]
    refs = refs[count + extra[1] :]
    send, receive, pair_send, pair_receive, local = refs[:5]
    size = len(order)
    me, ctx = lax.axis_index("fsdp"), lax.axis_index("ctx")
    core = lax.rem(ctx, 2)
    sibling = (me, ctx + 1 - 2 * core)
    inverse = [order.index(at) for at in range(size)]
    block = ring_blocks(order, pick(inverse, me))
    following, preceding = (block[1], ctx), (block[size - 1], ctx)
    line = ctx // 2
    peers = [(me, lax.rem(line + k, lines) * 2 + core) for k in range(1, lines)]
    greet([following, preceding, sibling] + (peers if side_in else []))
    started = []
    for a in range(count):
        copy = pltpu.make_async_copy(ins[a].at[core], outs[a].at[me, core], local.at[a])
        copy.start()
        started.append(copy)
    pending = []
    hooks = {}
    if side_in:
        hooks = attend_hooks(lines, ctx, sibling, peers, pending, side_in, side_out, refs[5:])
    hops = [(size // 2, size - 1 - size // 2), (size - 1 - size // 2, size // 2)]
    for step in range(size // 2 + 1):
        for a in range(count):
            for way in range(2):
                total = hops[a % 2][way]
                shift = (size - step) % size if way == 0 else step
                at = block[shift]
                source = outs[a].at[at, core] if step else ins[a].at[core]
                if 0 < step <= total:
                    remote(
                        source, source, send.at[a, way, step - 1],
                        receive.at[a, way, step - 1], following,
                    ).wait_recv()
                if step < total:
                    copy = remote(
                        source, outs[a].at[at, core], send.at[a, way, step],
                        receive.at[a, way, step], following if way == 0 else preceding,
                    )
                    copy.start()
                    pending.append(copy)
                if 0 < step <= total or (step == 0 and way == 0):
                    copy = remote(
                        source, outs[a].at[at, core], pair_send.at[a, shift],
                        pair_receive.at[a, shift], sibling,
                    )
                    copy.start()
                    pending.append(copy)
        if step in hooks:
            hooks[step]()
    for a in range(count):
        for shift in range(size):
            target = outs[a].at[block[shift], 1 - core]
            remote(
                target, target, pair_send.at[a, shift], pair_receive.at[a, shift], sibling
            ).wait_recv()
    for copy in pending:
        copy.wait_send()
    for copy in started:
        copy.wait()


def gather_all(shards, order, lines, collective_id, side=()):
    count, size = len(shards), len(order)
    dma = pltpu.SemaphoreType.DMA
    any_space = pl.BlockSpec(memory_space=pl.ANY)
    vmem = pl.BlockSpec(memory_space=pltpu.VMEM)
    side_out, sems = [], []
    if side:
        rows, width = side[2].shape
        side_out = [
            jax.ShapeDtypeStruct((2 * lines,) + side[3].shape, BF16),
            jax.ShapeDtypeStruct((rows, width), F32),
            jax.ShapeDtypeStruct((rows, LANES), F32),
        ]
        sems = [dma((max(lines - 1, 1),)), dma((max(lines - 1, 1),)), dma((lines,)), dma((lines,))]
    return pl.pallas_call(
        partial(gather_kernel, order, lines, count, (len(side), len(side_out))),
        out_shape=[jax.ShapeDtypeStruct((size,) + s.shape, s.dtype) for s in shards] + side_out,
        in_specs=[any_space] * count + [vmem] * len(side),
        out_specs=[any_space] * count + [vmem] * len(side_out),
        scratch_shapes=[
            dma((count, 2, size // 2)),
            dma((count, 2, size // 2)),
            dma((count, size)),
            dma((count, size)),
            dma((count,)),
        ]
        + sems,
        compiler_params=pltpu.CompilerParams(
            collective_id=collective_id, has_side_effects=True, vmem_limit_bytes=48 * 2**20
        ),
    )(*shards, *side)


def attend_back_hooks(lines, ctx, sibling, peers, pending, ins, outs, scratch):
    dq_ref, own_ref = outs
    dkv_ref, pair_ref, sum_ref, line_ref, pair_send, pair_receive, send, receive = scratch
    core, line = lax.rem(ctx, 2), ctx // 2
    groups = dq_ref.shape[1] // LANES

    def compute(third):
        span = range(third * groups // 3, (third + 1) * groups // 3)
        attend_back_part(span, *ins, dq_ref, dkv_ref)

    def begin():
        compute(2)
        for k in range(lines):
            at = lax.rem(line + k, lines)
            copy = remote(
                dkv_ref.at[2 * at + 1 - core], pair_ref.at[at],
                pair_send.at[k], pair_receive.at[k], sibling,
            )
            copy.start()
            pending.append(copy)

    def relay():
        for k in list(range(1, lines)) + [0]:
            at = lax.rem(line + k, lines)
            target = pair_ref.at[at]
            remote(target, target, pair_send.at[k], pair_receive.at[k], sibling).wait_recv()
            value = dkv_ref[2 * at + core].astype(F32) + pair_ref[at].astype(F32)
            sum_ref[k] = value.astype(BF16)
            if k:
                copy = remote(
                    sum_ref.at[k], line_ref.at[k - 1], send.at[k - 1], receive.at[k - 1],
                    peers[k - 1],
                )
                copy.start()
                pending.append(copy)

    def finish():
        value = sum_ref[0].astype(F32)
        for k in range(1, lines):
            target = line_ref.at[k - 1]
            remote(target, target, send.at[k - 1], receive.at[k - 1], peers[k - 1]).wait_recv()
            value = value + line_ref[k - 1].astype(F32)
        own_ref[...] = value.astype(BF16)

    return {0: partial(compute, 0), 1: partial(compute, 1), 2: begin, 4: relay, 7: finish}


def reduce_kernel(order, lines, count, extra, *refs):
    ins, side_in = refs[:count], refs[count : count + extra[0]]
    refs = refs[count + extra[0] :]
    outs, side_out = refs[:count], refs[count : count + extra[1]]
    refs = refs[count + extra[1] :]
    pairs, slots, crossed = refs[:count], refs[count : 2 * count], refs[2 * count : 3 * count]
    ring_send, ring_receive, pair_send, pair_receive = refs[3 * count : 3 * count + 4]
    line_send, line_receive, last_send, last_receive = refs[3 * count + 4 : 3 * count + 8]
    size = len(order)
    me, ctx = lax.axis_index("fsdp"), lax.axis_index("ctx")
    core = lax.rem(ctx, 2)
    line = ctx // 2
    sibling = (me, ctx + 1 - 2 * core)
    inverse = [order.index(at) for at in range(size)]
    block = ring_blocks(order, pick(inverse, me))
    ways = [(block[1], ctx), (block[size - 1], ctx)]
    peers = [(me, lax.rem(line + k, lines) * 2 + core) for k in range(1, lines)]
    greet(ways + [sibling] + peers)
    pending = []
    hooks = {}
    if side_in:
        side_scratch = refs[3 * count + 8 :]
        hooks = attend_back_hooks(
            lines, ctx, sibling, peers, pending, side_in, side_out, side_scratch
        )

    def shift_of(way, step):
        return (size - 1 - step) % size if way == 0 else (1 + step) % size

    ready = []
    for step in range(size):
        for way in range(2):
            shift = shift_of(way, step)
            if shift not in ready:
                ready.append(shift)
                for a in range(count):
                    copy = remote(
                        ins[a].at[block[shift], 1 - core], pairs[a].at[block[shift]],
                        pair_send.at[a, shift], pair_receive.at[a, shift], sibling,
                    )
                    copy.start()
                    pending.append(copy)
    waited = []

    def arrive(shift):
        if shift not in waited:
            waited.append(shift)
            for a in range(count):
                target = pairs[a].at[block[shift]]
                remote(
                    target, target, pair_send.at[a, shift], pair_receive.at[a, shift], sibling
                ).wait_recv()

    for step in range(size):
        for way in range(2):
            shift = shift_of(way, step)
            arrive(shift)
            at = block[shift]
            for a in range(count):
                half = ins[a].shape[3] // 2
                span = pl.ds(way * half, half)
                value = ins[a][at, core, :, span].astype(F32) + pairs[a][at, :, span].astype(F32)
                if step:
                    slot = slots[a].at[way, step - 1]
                    remote(
                        slot, slot, ring_send.at[a, way, step - 1],
                        ring_receive.at[a, way, step - 1], ways[way],
                    ).wait_recv()
                    value = value + slot[...].astype(F32)
                if step < size - 1:
                    held = slots[a].at[way, step - 1 if step else size - 1]
                    held[...] = value.astype(BF16)
                    copy = remote(
                        held, slots[a].at[way, step], ring_send.at[a, way, step],
                        ring_receive.at[a, way, step], ways[way],
                    )
                    copy.start()
                    pending.append(copy)
                else:
                    crossed[a][line, :, span] = value.astype(BF16)
        if step in hooks and step != 7:
            hooks[step]()
    for a in range(count):
        for k in range(1, lines):
            copy = remote(
                crossed[a].at[line], crossed[a].at[line], line_send.at[a, k - 1],
                line_receive.at[a, k - 1], peers[k - 1],
            )
            copy.start()
            pending.append(copy)
    if side_in:
        hooks[7]()
    for a in range(count):
        for k in range(1, lines):
            target = crossed[a].at[lax.rem(line + lines - k, lines)]
            remote(
                target, target, line_send.at[a, k - 1], line_receive.at[a, k - 1], peers[k - 1]
            ).wait_recv()
        value = crossed[a][0].astype(F32)
        for k in range(1, lines):
            value = value + crossed[a][k].astype(F32)
        outs[a][core] = value.astype(BF16)
        copy = remote(
            outs[a].at[core], outs[a].at[core], last_send.at[a], last_receive.at[a], sibling
        )
        copy.start()
        pending.append(copy)
    for a in range(count):
        target = outs[a].at[1 - core]
        remote(target, target, last_send.at[a], last_receive.at[a], sibling).wait_recv()
    for copy in pending:
        copy.wait_send()


def reduce_all(grads, order, lines, collective_id, side=()):
    count, size = len(grads), len(order)
    dma = pltpu.SemaphoreType.DMA
    vmem = pl.BlockSpec(memory_space=pltpu.VMEM)
    scratch = [pltpu.VMEM((size,) + g.shape[2:], BF16) for g in grads]
    scratch += [pltpu.VMEM((2, size, g.shape[2], g.shape[3] // 2), BF16) for g in grads]
    scratch += [pltpu.VMEM((lines,) + g.shape[2:], BF16) for g in grads]
    scratch += [dma((count, 2, size - 1)), dma((count, 2, size - 1))]
    scratch += [dma((count, size)), dma((count, size))]
    scratch += [dma((count, max(lines - 1, 1))), dma((count, max(lines - 1, 1)))]
    scratch += [dma((count,)), dma((count,))]
    side_out = []
    if side:
        rows, both = side[3].shape[1:]
        side_out = [
            jax.ShapeDtypeStruct(side[2].shape, BF16),
            jax.ShapeDtypeStruct((rows, both), BF16),
        ]
        scratch += [pltpu.VMEM((2 * lines, rows, both), BF16)]
        scratch += [pltpu.VMEM((lines, rows, both), BF16)] * 2
        scratch += [pltpu.VMEM((max(lines - 1, 1), rows, both), BF16)]
        scratch += [dma((lines,)), dma((lines,))]
        scratch += [dma((max(lines - 1, 1),)), dma((max(lines - 1, 1),))]
    return pl.pallas_call(
        partial(reduce_kernel, order, lines, count, (len(side), len(side_out))),
        out_shape=[jax.ShapeDtypeStruct(g.shape[1:], BF16) for g in grads] + side_out,
        in_specs=[vmem] * (count + len(side)),
        out_specs=[vmem] * (count + len(side_out)),
        scratch_shapes=scratch,
        compiler_params=pltpu.CompilerParams(
            collective_id=collective_id, has_side_effects=True, vmem_limit_bytes=56 * 2**20
        ),
    )(*grads, *side)


def round_up(value, unit):
    return -(-value // unit) * unit


def pad_to(array, shape):
    return jnp.pad(array, [(0, new - old) for old, new in zip(array.shape, shape)])


def shards(
    inputs,
    cotangent,
    block_order,
    norm1_gain,
    norm1_shift,
    w_qkv,
    qv_bias,
    w_out,
    out_bias,
    norm2_gain,
    norm2_shift,
    w_fc,
    fc_bias,
    w_proj,
    proj_bias,
):
    rows, width = inputs.shape[1:]
    positions = lax.axis_size("ctx")
    spread = lax.axis_size("fsdp")
    place = lax.axis_index("ctx")
    lines = positions // 2
    order = ring_order(spread, spread // lines if spread % lines == 0 else spread // 2)
    shard = width // spread
    sixteen = 16

    def two(weight):
        part = weight.shape[0] // 2
        weight = weight.reshape(2, part, weight.shape[1])
        return pad_to(weight, (2, round_up(part, sixteen), weight.shape[2]))

    def full(gathered, weight):
        part = weight.shape[0] // 2
        return gathered[:, :, :part].reshape(-1, weight.shape[1])

    def spread_out(grad):
        part = grad.shape[0] // spread // 2
        grad = grad.astype(BF16).reshape(spread, 2, part, grad.shape[1])
        return pad_to(grad, (spread, 2, round_up(part, sixteen), grad.shape[3]))

    def own(reduced, weight):
        part = weight.shape[0] // 2
        return reduced[:, :part].reshape(weight.shape).astype(F32)

    small = jnp.concatenate(
        [
            norm1_gain[None],
            norm1_shift[None],
            qv_bias,
            out_bias[None],
            norm2_gain[None],
            norm2_shift[None],
            proj_bias[None],
            fc_bias.reshape(-1, shard),
        ]
    )
    small_rows = small.shape[0]
    small = pad_to(small, (2 * sixteen, round_up(shard, LANES))).reshape(2, sixteen, -1)
    qkv_full, small = gather_all([two(w_qkv), small], order, lines, 0)
    qkv_full = full(qkv_full, w_qkv)
    small = small.reshape(spread, 2 * sixteen, -1)[:, :small_rows, :shard].astype(F32)
    vectors = jnp.moveaxis(small[:, :8], 0, 1).reshape(8, width)
    gain_one, shift_one, q_bias, v_bias, out_shift, gain_two, shift_two, proj_shift = vectors
    fc_shift = small[:, 8:].reshape(-1)

    tokens = inputs[0].astype(F32)
    unit_one, inverse_one = normalise(tokens)
    normed_one = (unit_one * gain_one + shift_one).astype(BF16)
    qkv_shift = jnp.concatenate([q_bias, jnp.zeros_like(q_bias), v_bias])
    qkv = (dot(normed_one, qkv_full) + qkv_shift).astype(BF16)
    q = qkv[:, :width]
    block_rows = rows * positions // block_order.shape[0]
    query_place = block_places(block_order, place * rows, rows, block_rows)[:, None]
    key_place = block_places(block_order, jnp.int32(0), rows * positions, block_rows)[None]
    fc_full, proj_full, out_full, kv, attended, logs = gather_all(
        [two(w_fc), two(w_proj), two(w_out)],
        order,
        lines,
        1,
        (query_place, key_place, q, qkv[:, width:]),
    )
    fc_full = full(fc_full, w_fc)
    proj_full = full(proj_full, w_proj)
    out_full = full(out_full, w_out)
    attended_low = attended.astype(BF16)
    middle = tokens + dot(attended_low, out_full) + out_shift
    unit_two, inverse_two = normalise(middle)
    normed_two = (unit_two * gain_two + shift_two).astype(BF16)
    hidden = dot(normed_two, fc_full) + fc_shift
    activated, slope = gelu_pair(hidden)
    activated = activated.astype(BF16)
    output = middle + dot(activated, proj_full) + proj_shift

    grad_output = cotangent[0]

    proj_grad = dot_rows(activated, grad_output)
    grad_hidden = (dot_lanes(grad_output, proj_full) * slope).astype(BF16)
    fc_grad = dot_rows(normed_two, grad_hidden)
    grad_normed_two = dot_lanes(grad_hidden, fc_full)
    grad_middle = grad_output.astype(F32) + norm_backward(
        grad_normed_two, gain_two, unit_two, inverse_two
    )
    grad_branch = grad_middle.astype(BF16)
    out_grad = dot_rows(attended_low, grad_branch)
    grad_attended = dot_lanes(grad_branch, out_full).astype(BF16)
    fc_grad, proj_grad, out_grad, dq, dkv = reduce_all(
        [spread_out(fc_grad), spread_out(proj_grad), spread_out(out_grad)],
        order,
        lines,
        2,
        (query_place, key_place, q, kv, attended, grad_attended, logs),
    )
    grad_qkv = jnp.concatenate([dq, dkv], axis=1)
    qkv_grad = dot_rows(normed_one, grad_qkv)
    grad_normed_one = dot_lanes(grad_qkv, qkv_full)
    grad_tokens = grad_middle + norm_backward(grad_normed_one, gain_one, unit_one, inverse_one)

    def total(values):
        return jnp.sum(values, axis=0, dtype=F32)

    columns = total(grad_qkv)
    small_grad = jnp.stack(
        [
            total(grad_normed_one * unit_one),
            total(grad_normed_one),
            columns[:width],
            columns[2 * width :],
            total(grad_branch),
            total(grad_normed_two * unit_two),
            total(grad_normed_two),
            total(grad_output),
        ]
    )
    small_grad = jnp.moveaxis(small_grad.reshape(8, spread, shard), 1, 0)
    small_grad = jnp.concatenate(
        [small_grad, total(grad_hidden).reshape(spread, -1, shard)], axis=1
    )
    small_grad = pad_to(
        small_grad, (spread, 2 * sixteen, round_up(shard, 2 * LANES))
    ).reshape(spread, 2, sixteen, -1)
    qkv_grad, small_grad = reduce_all(
        [spread_out(qkv_grad), small_grad.astype(BF16)], order, lines, 3
    )
    small_grad = small_grad.reshape(2 * sixteen, -1)[:small_rows, :shard].astype(F32)

    return (
        output[None].astype(BF16),
        grad_tokens[None].astype(BF16),
        small_grad[0],
        small_grad[1],
        own(qkv_grad, w_qkv),
        small_grad[2:4],
        own(out_grad, w_out),
        small_grad[4],
        small_grad[5],
        small_grad[6],
        own(fc_grad, w_fc),
        small_grad[8:].reshape(-1),
        own(proj_grad, w_proj),
        small_grad[7],
    )


def solution(mesh):
    in_specs = (
        P("fsdp", "ctx", None),
        P("fsdp", "ctx", None),
        P(),
        P("fsdp"),
        P("fsdp"),
        P("fsdp", None),
        P(None, "fsdp"),
        P("fsdp", None),
        P("fsdp"),
        P("fsdp"),
        P("fsdp"),
        P("fsdp", None),
        P("fsdp"),
        P("fsdp", None),
        P("fsdp"),
    )
    out_specs = (
        P("fsdp", "ctx", None),
        P("fsdp", "ctx", None),
        P("fsdp"),
        P("fsdp"),
        P("fsdp", None),
        P(None, "fsdp"),
        P("fsdp", None),
        P("fsdp"),
        P("fsdp"),
        P("fsdp"),
        P("fsdp", None),
        P("fsdp"),
        P("fsdp", None),
        P("fsdp"),
    )
    return jax.shard_map(shards, mesh=mesh, in_specs=in_specs, out_specs=out_specs, check_vma=False)
```

```python
from functools import partial

import jax
import jax.numpy as jnp
from jax import lax
from jax.experimental import pallas as pl
from jax.experimental.pallas import tpu as pltpu
from jax.sharding import PartitionSpec as P

HEADS = 12
EPS = 1e-05
LOWEST = -1e30
LANES = 128
F32 = jnp.float32
BF16 = jnp.bfloat16
ROW_DOT = (((0,), (0,)), ((), ()))
LANE_DOT = (((1,), (1,)), ((), ()))


def dot(left, right):
    return jnp.dot(left, right, preferred_element_type=F32)


def dot_rows(left, right):
    return lax.dot_general(left, right, ROW_DOT, preferred_element_type=F32)


def dot_lanes(left, right):
    return lax.dot_general(left, right, LANE_DOT, preferred_element_type=F32)


def normalise(values):
    centred = values - jnp.mean(values, axis=-1, keepdims=True)
    spread = jnp.mean(centred * centred, axis=-1, keepdims=True)
    inverse = lax.rsqrt(spread + EPS)
    return centred * inverse, inverse


def norm_backward(incoming, gain, unit, inverse):
    scaled = incoming * gain
    first = jnp.mean(scaled, axis=-1, keepdims=True)
    second = jnp.mean(scaled * unit, axis=-1, keepdims=True)
    return inverse * (scaled - first - unit * second)


def gelu_pair(values):
    inner = 0.7978845608028654 * (values + 0.044715 * values * values * values)
    bent = jnp.tanh(inner)
    slope = 0.7978845608028654 * (1.0 + 0.134145 * values * values)
    value = 0.5 * values * (1.0 + bent)
    derivative = 0.5 * (1.0 + bent) + 0.5 * values * (1.0 - bent * bent) * slope
    return value, derivative


def block_places(block_order, first_row, row_count, block_rows):
    row_index = first_row + jnp.arange(row_count, dtype=jnp.int32)
    which_block = row_index // block_rows
    table = jnp.arange(block_order.shape[0], dtype=jnp.int32)
    picked = jnp.sum(
        jnp.where(which_block[:, None] == table[None, :], block_order[None, :], 0), axis=1
    )
    return picked * block_rows + row_index % block_rows


def attend_part(query_place, key_place, q_ref, kv_ref, out_ref, log_ref):
    rows, width = q_ref.shape
    head_dim = width // HEADS
    per_group = LANES // head_dim
    visible = key_place[...] <= query_place[...]
    lane = lax.broadcasted_iota(jnp.int32, (rows, LANES), 1)
    logs = jnp.zeros((rows, LANES), F32)
    for group in range(width // LANES):
        span = pl.ds(group * LANES, LANES)
        q = q_ref[:, span] * (head_dim**-0.5)
        k = kv_ref[:, :, span].reshape(-1, LANES)
        v = kv_ref[:, :, pl.ds(width + group * LANES, LANES)].reshape(-1, LANES)
        out = jnp.zeros((rows, LANES), F32)
        for part in range(per_group):
            own = lane // head_dim == part
            scores = dot_lanes(jnp.where(own, q, jnp.zeros_like(q)), k)
            scores = jnp.where(visible, scores, LOWEST)
            high = jnp.max(scores, axis=1, keepdims=True)
            shares = jnp.exp(scores - high)
            total = jnp.sum(shares, axis=1, keepdims=True)
            out = jnp.where(own, dot(shares.astype(BF16), v) / total, out)
            logs = jnp.where(lane == group * per_group + part, high + jnp.log(total), logs)
        out_ref[:, span] = out
    log_ref[...] = logs


def attend_back_part(
    groups, query_place, key_place, q_ref, kv_ref, att_ref, grad_ref, log_ref, dq_ref, dkv_ref
):
    rows, width = q_ref.shape
    head_dim = width // HEADS
    per_group = LANES // head_dim
    scale = head_dim**-0.5
    visible = key_place[...] <= query_place[...]
    lane = lax.broadcasted_iota(jnp.int32, (rows, LANES), 1)
    for group in groups:
        span = pl.ds(group * LANES, LANES)
        far = pl.ds(width + group * LANES, LANES)
        q = q_ref[:, span] * scale
        k = kv_ref[:, :, span].reshape(-1, LANES)
        v = kv_ref[:, :, far].reshape(-1, LANES)
        grad = grad_ref[:, span]
        product = grad.astype(F32) * att_ref[:, span]
        dq = jnp.zeros((rows, LANES), F32)
        dk = jnp.zeros((k.shape[0], LANES), F32)
        dv = jnp.zeros((k.shape[0], LANES), F32)
        for part in range(per_group):
            own = lane // head_dim == part
            own_q = jnp.where(own, q, jnp.zeros_like(q))
            own_grad = jnp.where(own, grad, jnp.zeros_like(grad))
            delta = jnp.sum(jnp.where(own, product, 0.0), axis=1, keepdims=True)
            log = jnp.sum(
                jnp.where(lane == group * per_group + part, log_ref[...], 0.0),
                axis=1,
                keepdims=True,
            )
            scores = jnp.where(visible, dot_lanes(own_q, k), LOWEST)
            shares = jnp.exp(scores - log)
            dv = dv + dot_rows(shares.astype(BF16), own_grad)
            change = (shares * (dot_lanes(own_grad, v) - delta)).astype(BF16)
            dq = jnp.where(own, dot(change, k) * scale, dq)
            dk = dk + dot_rows(change, own_q)
        dq_ref[:, span] = dq.astype(BF16)
        shape = (kv_ref.shape[0], rows, LANES)
        dkv_ref[:, :, span] = dk.astype(BF16).reshape(shape)
        dkv_ref[:, :, far] = dv.astype(BF16).reshape(shape)


MESH = pl.DeviceIdType.MESH


def ring_order(fsdp, depth):
    across = fsdp // depth
    order = []
    for z in range(depth):
        columns = list(range(1, across))
        order += [z * across + y for y in (columns if z % 2 == 0 else columns[::-1])]
    return order + [z * across for z in range(depth - 1, -1, -1)]


def pick(table, index):
    found = jnp.int32(table[0])
    for at in range(1, len(table)):
        found = jnp.where(index == at, jnp.int32(table[at]), found)
    return found


def ring_blocks(order, position):
    size = len(order)
    return [pick(order, lax.rem(position + shift, size)) for shift in range(size)]


def remote(source, target, send, receive, device):
    return pltpu.make_async_remote_copy(
        src_ref=source,
        dst_ref=target,
        send_sem=send,
        recv_sem=receive,
        device_id=device,
        device_id_type=MESH,
    )


def greet(devices):
    barrier = pltpu.get_barrier_semaphore()
    for device in devices:
        pl.semaphore_signal(barrier, inc=1, device_id=device, device_id_type=MESH)
    pl.semaphore_wait(barrier, len(devices))


def attend_hooks(lines, ctx, sibling, peers, pending, ins, outs, sems):
    query_place, key_place, q_ref, own_ref = ins
    kv_ref, out_ref, log_ref = outs
    send, receive, pair_send, pair_receive = sems
    core, line = lax.rem(ctx, 2), ctx // 2

    def to_sibling(source, at, slot):
        copy = remote(source, kv_ref.at[at], pair_send.at[slot], pair_receive.at[slot], sibling)
        copy.start()
        pending.append(copy)

    def begin():
        for k in range(1, lines):
            copy = remote(
                own_ref, kv_ref.at[ctx], send.at[k - 1], receive.at[k - 1], peers[k - 1]
            )
            copy.start()
            pending.append(copy)
        to_sibling(own_ref, ctx, 0)
        kv_ref[ctx] = own_ref[...]

    def relay():
        for k in range(1, lines):
            at = lax.rem(line + lines - k, lines) * 2 + core
            target = kv_ref.at[at]
            remote(target, target, send.at[k - 1], receive.at[k - 1], peers[k - 1]).wait_recv()
            to_sibling(target, at, k)

    def compute():
        for k in range(lines):
            target = kv_ref.at[lax.rem(line + lines - k, lines) * 2 + 1 - core]
            remote(target, target, pair_send.at[k], pair_receive.at[k], sibling).wait_recv()
        attend_part(query_place, key_place, q_ref, kv_ref, out_ref, log_ref)

    return {0: begin, 1: relay, 2: compute}


def gather_kernel(order, lines, count, extra, *refs):
    ins, side_in = refs[:count], refs[count : count + extra[0]]
    refs = refs[count + extra[0] :]
    outs, side_out = refs[:count], refs[count : count + extra[1]]
    refs = refs[count + extra[1] :]
    send, receive, pair_send, pair_receive, local = refs[:5]
    size = len(order)
    me, ctx = lax.axis_index("fsdp"), lax.axis_index("ctx")
    core = lax.rem(ctx, 2)
    sibling = (me, ctx + 1 - 2 * core)
    inverse = [order.index(at) for at in range(size)]
    block = ring_blocks(order, pick(inverse, me))
    following, preceding = (block[1], ctx), (block[size - 1], ctx)
    line = ctx // 2
    peers = [(me, lax.rem(line + k, lines) * 2 + core) for k in range(1, lines)]
    greet([following, preceding, sibling] + (peers if side_in else []))
    started = []
    for a in range(count):
        copy = pltpu.make_async_copy(ins[a].at[core], outs[a].at[me, core], local.at[a])
        copy.start()
        started.append(copy)
    pending = []
    hooks = {}
    if side_in:
        hooks = attend_hooks(lines, ctx, sibling, peers, pending, side_in, side_out, refs[5:])
    hops = [(size // 2, size - 1 - size // 2), (size - 1 - size // 2, size // 2)]
    for step in range(size // 2 + 1):
        for a in range(count):
            for way in range(2):
                total = hops[a % 2][way]
                shift = (size - step) % size if way == 0 else step
                at = block[shift]
                source = outs[a].at[at, core] if step else ins[a].at[core]
                if 0 < step <= total:
                    remote(
                        source, source, send.at[a, way, step - 1],
                        receive.at[a, way, step - 1], following,
                    ).wait_recv()
                if step < total:
                    copy = remote(
                        source, outs[a].at[at, core], send.at[a, way, step],
                        receive.at[a, way, step], following if way == 0 else preceding,
                    )
                    copy.start()
                    pending.append(copy)
                if 0 < step <= total or (step == 0 and way == 0):
                    copy = remote(
                        source, outs[a].at[at, core], pair_send.at[a, shift],
                        pair_receive.at[a, shift], sibling,
                    )
                    copy.start()
                    pending.append(copy)
        if step in hooks:
            hooks[step]()
    for a in range(count):
        for shift in range(size):
            target = outs[a].at[block[shift], 1 - core]
            remote(
                target, target, pair_send.at[a, shift], pair_receive.at[a, shift], sibling
            ).wait_recv()
    for copy in pending:
        copy.wait_send()
    for copy in started:
        copy.wait()


def gather_all(shards, order, lines, collective_id, side=()):
    count, size = len(shards), len(order)
    dma = pltpu.SemaphoreType.DMA
    any_space = pl.BlockSpec(memory_space=pl.ANY)
    vmem = pl.BlockSpec(memory_space=pltpu.VMEM)
    side_out, sems = [], []
    if side:
        rows, width = side[2].shape
        side_out = [
            jax.ShapeDtypeStruct((2 * lines,) + side[3].shape, BF16),
            jax.ShapeDtypeStruct((rows, width), F32),
            jax.ShapeDtypeStruct((rows, LANES), F32),
        ]
        sems = [dma((max(lines - 1, 1),)), dma((max(lines - 1, 1),)), dma((lines,)), dma((lines,))]
    return pl.pallas_call(
        partial(gather_kernel, order, lines, count, (len(side), len(side_out))),
        out_shape=[jax.ShapeDtypeStruct((size,) + s.shape, s.dtype) for s in shards] + side_out,
        in_specs=[any_space] * count + [vmem] * len(side),
        out_specs=[any_space] * count + [vmem] * len(side_out),
        scratch_shapes=[
            dma((count, 2, size // 2)),
            dma((count, 2, size // 2)),
            dma((count, size)),
            dma((count, size)),
            dma((count,)),
        ]
        + sems,
        compiler_params=pltpu.CompilerParams(
            collective_id=collective_id, has_side_effects=True, vmem_limit_bytes=48 * 2**20
        ),
    )(*shards, *side)


def attend_back_hooks(lines, ctx, sibling, peers, pending, ins, outs, scratch):
    dq_ref, own_ref = outs
    dkv_ref, pair_ref, sum_ref, line_ref, pair_send, pair_receive, send, receive = scratch
    core, line = lax.rem(ctx, 2), ctx // 2
    groups = dq_ref.shape[1] // LANES

    def compute(third):
        span = range(third * groups // 3, (third + 1) * groups // 3)
        attend_back_part(span, *ins, dq_ref, dkv_ref)

    def begin():
        compute(2)
        for k in range(lines):
            at = lax.rem(line + k, lines)
            copy = remote(
                dkv_ref.at[2 * at + 1 - core], pair_ref.at[at],
                pair_send.at[k], pair_receive.at[k], sibling,
            )
            copy.start()
            pending.append(copy)

    def relay():
        for k in list(range(1, lines)) + [0]:
            at = lax.rem(line + k, lines)
            target = pair_ref.at[at]
            remote(target, target, pair_send.at[k], pair_receive.at[k], sibling).wait_recv()
            value = dkv_ref[2 * at + core].astype(F32) + pair_ref[at].astype(F32)
            sum_ref[k] = value.astype(BF16)
            if k:
                copy = remote(
                    sum_ref.at[k], line_ref.at[k - 1], send.at[k - 1], receive.at[k - 1],
                    peers[k - 1],
                )
                copy.start()
                pending.append(copy)

    def finish():
        value = sum_ref[0].astype(F32)
        for k in range(1, lines):
            target = line_ref.at[k - 1]
            remote(target, target, send.at[k - 1], receive.at[k - 1], peers[k - 1]).wait_recv()
            value = value + line_ref[k - 1].astype(F32)
        own_ref[...] = value.astype(BF16)

    return {0: partial(compute, 0), 1: partial(compute, 1), 2: begin, 4: relay, 7: finish}


def reduce_kernel(order, lines, count, carried, extra, *refs):
    carry, refs = refs[:carried], refs[carried:]
    ins, side_in = refs[:count], refs[count : count + extra[0]]
    refs = refs[count + extra[0] :]
    final = not side_in
    made = count + carried
    outs, side_out = refs[:made], refs[made : made + extra[1]]
    refs = refs[made + extra[1] :]
    pairs, slots, refs = refs[:count], refs[count : 2 * count], refs[2 * count :]
    ring_send, ring_receive, pair_send, pair_receive = refs[:4]
    refs = refs[4:]
    if final:
        line_send, line_receive, last_send, last_receive = refs[:4]
        crossed = refs[4:]
    size = len(order)
    me, ctx = lax.axis_index("fsdp"), lax.axis_index("ctx")
    core = lax.rem(ctx, 2)
    line = ctx // 2
    sibling = (me, ctx + 1 - 2 * core)
    inverse = [order.index(at) for at in range(size)]
    block = ring_blocks(order, pick(inverse, me))
    ways = [(block[1], ctx), (block[size - 1], ctx)]
    peers = [(me, lax.rem(line + k, lines) * 2 + core) for k in range(1, lines)]
    greet(ways + [sibling] + peers)
    pending = []
    hooks = {}
    if side_in:
        hooks = attend_back_hooks(lines, ctx, sibling, peers, pending, side_in, side_out, refs)

    def send_lines(a):
        for k in range(1, lines):
            copy = remote(
                crossed[a].at[line], crossed[a].at[line], line_send.at[a, k - 1],
                line_receive.at[a, k - 1], peers[k - 1],
            )
            copy.start()
            pending.append(copy)

    def sum_lines(a):
        for k in range(1, lines):
            target = crossed[a].at[lax.rem(line + lines - k, lines)]
            remote(
                target, target, line_send.at[a, k - 1], line_receive.at[a, k - 1], peers[k - 1]
            ).wait_recv()
        value = crossed[a][0].astype(F32)
        for k in range(1, lines):
            value = value + crossed[a][k].astype(F32)
        outs[a][core] = value.astype(BF16)
        copy = remote(
            outs[a].at[core], outs[a].at[core], last_send.at[a], last_receive.at[a], sibling
        )
        copy.start()
        pending.append(copy)

    def shift_of(way, step):
        return (size - 1 - step) % size if way == 0 else (1 + step) % size

    ready = []
    for step in range(size):
        for way in range(2):
            shift = shift_of(way, step)
            if shift not in ready:
                ready.append(shift)
                for a in range(count):
                    copy = remote(
                        ins[a].at[block[shift], 1 - core], pairs[a].at[block[shift]],
                        pair_send.at[a, shift], pair_receive.at[a, shift], sibling,
                    )
                    copy.start()
                    pending.append(copy)
    for a in range(count, made):
        crossed[a][line] = carry[a - count][...]
        send_lines(a)
    waited = []

    def arrive(shift):
        if shift not in waited:
            waited.append(shift)
            for a in range(count):
                target = pairs[a].at[block[shift]]
                remote(
                    target, target, pair_send.at[a, shift], pair_receive.at[a, shift], sibling
                ).wait_recv()

    for step in range(size):
        for way in range(2):
            shift = shift_of(way, step)
            arrive(shift)
            at = block[shift]
            for a in range(count):
                half = ins[a].shape[3] // 2
                span = pl.ds(way * half, half)
                value = ins[a][at, core, :, span].astype(F32) + pairs[a][at, :, span].astype(F32)
                if step:
                    slot = slots[a].at[way, step - 1]
                    remote(
                        slot, slot, ring_send.at[a, way, step - 1],
                        ring_receive.at[a, way, step - 1], ways[way],
                    ).wait_recv()
                    value = value + slot[...].astype(F32)
                if step < size - 1:
                    held = slots[a].at[way, step - 1 if step else size - 1]
                    held[...] = value.astype(BF16)
                    copy = remote(
                        held, slots[a].at[way, step], ring_send.at[a, way, step],
                        ring_receive.at[a, way, step], ways[way],
                    )
                    copy.start()
                    pending.append(copy)
                elif final:
                    crossed[a][line, :, span] = value.astype(BF16)
                else:
                    outs[a][:, span] = value.astype(BF16)
        if step in hooks and step != 7:
            hooks[step]()
        if step == size - 2:
            for a in range(count, made):
                sum_lines(a)
    if side_in:
        hooks[7]()
    if final:
        for a in range(count):
            send_lines(a)
        for a in range(count):
            sum_lines(a)
        for a in range(made):
            target = outs[a].at[1 - core]
            remote(target, target, last_send.at[a], last_receive.at[a], sibling).wait_recv()
    for copy in pending:
        copy.wait_send()


def reduce_all(grads, order, lines, collective_id, side=(), carry=()):
    count, size = len(grads), len(order)
    dma = pltpu.SemaphoreType.DMA
    vmem = pl.BlockSpec(memory_space=pltpu.VMEM)
    scratch = [pltpu.VMEM((size,) + g.shape[2:], BF16) for g in grads]
    scratch += [pltpu.VMEM((2, size, g.shape[2], g.shape[3] // 2), BF16) for g in grads]
    scratch += [dma((count, 2, size - 1)), dma((count, 2, size - 1))]
    scratch += [dma((count, size)), dma((count, size))]
    made = count + len(carry)
    parts = [g.shape[2:] for g in grads] + [c.shape for c in carry]
    if not side:
        scratch += [dma((made, max(lines - 1, 1))), dma((made, max(lines - 1, 1)))]
        scratch += [dma((made,)), dma((made,))]
        scratch += [pltpu.VMEM((lines,) + part, BF16) for part in parts]
        parts = [(2,) + part for part in parts]
    side_out = []
    if side:
        rows, both = side[3].shape[1:]
        side_out = [
            jax.ShapeDtypeStruct(side[2].shape, BF16),
            jax.ShapeDtypeStruct((rows, both), BF16),
        ]
        scratch += [pltpu.VMEM((2 * lines, rows, both), BF16)]
        scratch += [pltpu.VMEM((lines, rows, both), BF16)] * 2
        scratch += [pltpu.VMEM((max(lines - 1, 1), rows, both), BF16)]
        scratch += [dma((lines,)), dma((lines,))]
        scratch += [dma((max(lines - 1, 1),)), dma((max(lines - 1, 1),))]
    return pl.pallas_call(
        partial(reduce_kernel, order, lines, count, len(carry), (len(side), len(side_out))),
        out_shape=[jax.ShapeDtypeStruct(part, BF16) for part in parts] + side_out,
        in_specs=[vmem] * (made + len(side)),
        out_specs=[vmem] * (made + len(side_out)),
        scratch_shapes=scratch,
        compiler_params=pltpu.CompilerParams(
            collective_id=collective_id, has_side_effects=True, vmem_limit_bytes=56 * 2**20
        ),
    )(*carry, *grads, *side)


def round_up(value, unit):
    return -(-value // unit) * unit


def pad_to(array, shape):
    return jnp.pad(array, [(0, new - old) for old, new in zip(array.shape, shape)])


def shards(
    inputs,
    cotangent,
    block_order,
    norm1_gain,
    norm1_shift,
    w_qkv,
    qv_bias,
    w_out,
    out_bias,
    norm2_gain,
    norm2_shift,
    w_fc,
    fc_bias,
    w_proj,
    proj_bias,
):
    rows, width = inputs.shape[1:]
    positions = lax.axis_size("ctx")
    spread = lax.axis_size("fsdp")
    place = lax.axis_index("ctx")
    lines = positions // 2
    order = ring_order(spread, spread // lines if spread % lines == 0 else spread // 2)
    shard = width // spread
    sixteen = 16

    def two(weight):
        part = weight.shape[0] // 2
        weight = weight.reshape(2, part, weight.shape[1])
        return pad_to(weight, (2, round_up(part, sixteen), weight.shape[2]))

    def full(gathered, weight):
        part = weight.shape[0] // 2
        return gathered[:, :, :part].reshape(-1, weight.shape[1])

    def spread_out(grad):
        part = grad.shape[0] // spread // 2
        grad = grad.astype(BF16).reshape(spread, 2, part, grad.shape[1])
        return pad_to(grad, (spread, 2, round_up(part, sixteen), grad.shape[3]))

    def own(reduced, weight):
        part = weight.shape[0] // 2
        return reduced[:, :part].reshape(weight.shape).astype(F32)

    small = jnp.concatenate(
        [
            norm1_gain[None],
            norm1_shift[None],
            qv_bias,
            out_bias[None],
            norm2_gain[None],
            norm2_shift[None],
            proj_bias[None],
            fc_bias.reshape(-1, shard),
        ]
    )
    small_rows = small.shape[0]
    small = pad_to(small, (2 * sixteen, round_up(shard, LANES))).reshape(2, sixteen, -1)
    qkv_full, small = gather_all([two(w_qkv), small], order, lines, 0)
    qkv_full = full(qkv_full, w_qkv)
    small = small.reshape(spread, 2 * sixteen, -1)[:, :small_rows, :shard].astype(F32)
    vectors = jnp.moveaxis(small[:, :8], 0, 1).reshape(8, width)
    gain_one, shift_one, q_bias, v_bias, out_shift, gain_two, shift_two, proj_shift = vectors
    fc_shift = small[:, 8:].reshape(-1)

    tokens = inputs[0].astype(F32)
    unit_one, inverse_one = normalise(tokens)
    normed_one = (unit_one * gain_one + shift_one).astype(BF16)
    qkv_shift = jnp.concatenate([q_bias, jnp.zeros_like(q_bias), v_bias])
    qkv = (dot(normed_one, qkv_full) + qkv_shift).astype(BF16)
    q = qkv[:, :width]
    block_rows = rows * positions // block_order.shape[0]
    query_place = block_places(block_order, place * rows, rows, block_rows)[:, None]
    key_place = block_places(block_order, jnp.int32(0), rows * positions, block_rows)[None]
    fc_full, proj_full, out_full, kv, attended, logs = gather_all(
        [two(w_fc), two(w_proj), two(w_out)],
        order,
        lines,
        1,
        (query_place, key_place, q, qkv[:, width:]),
    )
    fc_full = full(fc_full, w_fc)
    proj_full = full(proj_full, w_proj)
    out_full = full(out_full, w_out)
    attended_low = attended.astype(BF16)
    middle = tokens + dot(attended_low, out_full) + out_shift
    unit_two, inverse_two = normalise(middle)
    normed_two = (unit_two * gain_two + shift_two).astype(BF16)
    hidden = dot(normed_two, fc_full) + fc_shift
    activated, slope = gelu_pair(hidden)
    activated = activated.astype(BF16)
    output = middle + dot(activated, proj_full) + proj_shift

    grad_output = cotangent[0]

    proj_grad = dot_rows(activated, grad_output)
    grad_hidden = (dot_lanes(grad_output, proj_full) * slope).astype(BF16)
    fc_grad = dot_rows(normed_two, grad_hidden)
    grad_normed_two = dot_lanes(grad_hidden, fc_full)
    grad_middle = grad_output.astype(F32) + norm_backward(
        grad_normed_two, gain_two, unit_two, inverse_two
    )
    grad_branch = grad_middle.astype(BF16)
    out_grad = dot_rows(attended_low, grad_branch)
    grad_attended = dot_lanes(grad_branch, out_full).astype(BF16)
    fc_grad, proj_grad, out_grad, dq, dkv = reduce_all(
        [spread_out(fc_grad), spread_out(proj_grad), spread_out(out_grad)],
        order,
        lines,
        2,
        (query_place, key_place, q, kv, attended, grad_attended, logs),
    )
    grad_qkv = jnp.concatenate([dq, dkv], axis=1)
    qkv_grad = dot_rows(normed_one, grad_qkv)
    grad_normed_one = dot_lanes(grad_qkv, qkv_full)
    grad_tokens = grad_middle + norm_backward(grad_normed_one, gain_one, unit_one, inverse_one)

    def total(values):
        return jnp.sum(values, axis=0, dtype=F32)

    columns = total(grad_qkv)
    small_grad = jnp.stack(
        [
            total(grad_normed_one * unit_one),
            total(grad_normed_one),
            columns[:width],
            columns[2 * width :],
            total(grad_branch),
            total(grad_normed_two * unit_two),
            total(grad_normed_two),
            total(grad_output),
        ]
    )
    small_grad = jnp.moveaxis(small_grad.reshape(8, spread, shard), 1, 0)
    small_grad = jnp.concatenate(
        [small_grad, total(grad_hidden).reshape(spread, -1, shard)], axis=1
    )
    small_grad = pad_to(
        small_grad, (spread, 2 * sixteen, round_up(shard, 2 * LANES))
    ).reshape(spread, 2, sixteen, -1)
    qkv_grad, small_grad, fc_grad, proj_grad, out_grad = reduce_all(
        [spread_out(qkv_grad), small_grad.astype(BF16)],
        order,
        lines,
        3,
        carry=(fc_grad, proj_grad, out_grad),
    )
    small_grad = small_grad.reshape(2 * sixteen, -1)[:small_rows, :shard].astype(F32)

    return (
        output[None].astype(BF16),
        grad_tokens[None].astype(BF16),
        small_grad[0],
        small_grad[1],
        own(qkv_grad, w_qkv),
        small_grad[2:4],
        own(out_grad, w_out),
        small_grad[4],
        small_grad[5],
        small_grad[6],
        own(fc_grad, w_fc),
        small_grad[8:].reshape(-1),
        own(proj_grad, w_proj),
        small_grad[7],
    )


def solution(mesh):
    in_specs = (
        P("fsdp", "ctx", None),
        P("fsdp", "ctx", None),
        P(),
        P("fsdp"),
        P("fsdp"),
        P("fsdp", None),
        P(None, "fsdp"),
        P("fsdp", None),
        P("fsdp"),
        P("fsdp"),
        P("fsdp"),
        P("fsdp", None),
        P("fsdp"),
        P("fsdp", None),
        P("fsdp"),
    )
    out_specs = (
        P("fsdp", "ctx", None),
        P("fsdp", "ctx", None),
        P("fsdp"),
        P("fsdp"),
        P("fsdp", None),
        P(None, "fsdp"),
        P("fsdp", None),
        P("fsdp"),
        P("fsdp"),
        P("fsdp"),
        P("fsdp", None),
        P("fsdp"),
        P("fsdp", None),
        P("fsdp"),
    )
    return jax.shard_map(shards, mesh=mesh, in_specs=in_specs, out_specs=out_specs, check_vma=False)
```
